32 devices in a mesh: groups: 2 (over x), segment: 2 (over core), block: 8 (over z, y).
Axes of the slice: x: 2, y: 2, z: 4, core: 2. Of those that a mesh axis runs over, the one named last changes fastest.
Arguments:
- tokens: float32 [1024, 16384], P(('groups', 'segment'), 'block'), parts along dimension 0, may hold values from -32 to 32
- gains: float32 [2, 2, 16384], P('segment', None, 'block'), may hold values from 0.1 to 1.9
- right_factors: float32 [2, 2, 128, 128, 128], P('segment', None, 'block'), may hold values from -0.5 to 0.5
- left_factors: float32 [2, 2, 128, 128, 128], P('segment', None, 'block'), may hold values from -0.5 to 0.5
Outputs:
- output: float32 [1024, 16384], P(('groups', 'segment'), 'block'), parts along dimension 0
The draws below stay inside these ranges and needn't reach their ends.
There are 2 independent parts, one for each index of `groups`. The reference program is written for one: setup_inputs(seed, part) draws one part's arguments, and reference() takes and returns one part's arrays. A program takes and returns all parts, laid end to end along the dimension named above; an argument that names none is the same for every part. Nothing has to cross between parts.
All inputs are finite; a program needn't handle non-finite values.
Results may differ from the reference program's by a relative error of at most 0.0003.
Values sent between devices are 32-bit elements; how exact they have to be, the bound alone decides.
No kernel may reach another device: no remote copies, remote signals or barrier semaphores. Data moves between devices by JAX's collectives and lax.ppermute only.
A program may use at most 64 MiB of HBM per device.

```python
import math
import jax
import jax.numpy as jnp
from jax import lax

NB = 128
BS = 128
D = 16384
ROUNDS = 2
TOKENS = 512
N_SEGMENT = 2


def draw_tokens(key, part):
    first_key, second_key = jax.random.split(key, 2)
    position = jnp.arange(D, dtype=jnp.float32) / (D - 1)
    values = jnp.clip(jax.random.normal(first_key, (TOKENS, D), jnp.float32), -5.0, 5.0)
    column_scale = 0.3 * jnp.exp(position * math.log(10.0))
    row_scale = jnp.exp(jax.random.uniform(second_key, (TOKENS, 1), jnp.float32, math.log(0.6), math.log(1.8)))
    return (values * row_scale * column_scale[None, :]).astype(jnp.float32)


def level_of(stream_key, extent, cuts, least, largest):
    loudness = 1.0
    for dim, parts in cuts:
        draws = jax.random.uniform(jax.random.fold_in(jax.random.fold_in(stream_key, 6), dim), (parts,), jnp.float32, least / len(cuts), largest / len(cuts))
        loudness = loudness * jnp.repeat(jnp.exp(draws), extent[dim] // parts).reshape((-1,) + (1,) * (len(extent) - 1 - dim))
    return loudness


def noise(key, extent, width, limit, cuts=(), kind=jnp.bfloat16):
    drawn = width * jax.random.normal(key, extent, jnp.float32)
    if cuts:
        drawn = drawn * level_of(key, extent, cuts, -0.22, 0.18)
    return jnp.clip(drawn, -limit, limit).astype(kind)


def setup_inputs(seed: int = 0, part: int = 0) -> dict:
    splits = jax.random.split(jax.random.key(seed), 5)
    own_keys = jax.random.split(jax.random.fold_in(splits[4], part), 5)
    tokens = draw_tokens(jax.random.fold_in(jax.random.fold_in(splits[4], part), 71), part)
    gains = jnp.clip(1.0 + 0.18 * jax.random.normal(splits[1], (N_SEGMENT, ROUNDS, D), jnp.float32), 0.1, 1.9)
    right_factors = noise(splits[2], (N_SEGMENT, ROUNDS, NB, BS, BS), BS ** -0.5, 0.5, ((0, 2), (2, 8)), jnp.float32)
    left_factors = noise(splits[3], (N_SEGMENT, ROUNDS, BS, NB, NB), NB ** -0.5, 0.5, ((0, 2), (2, 8)), jnp.float32)
    return {"tokens": tokens, "gains": gains, "right_factors": right_factors, "left_factors": left_factors}


epsilon = 1e-06

def one_layer(current, gain_row, right_part, left_part):
    sum_squares = lax.optimization_barrier(jnp.sum(current * current, axis=1, keepdims=True))
    normed = current * lax.rsqrt(sum_squares / D + epsilon) * gain_row[None, :]
    inner = jnp.einsum('tbi,bij->tbj', normed.reshape(-1, NB, BS), right_part, precision=lax.Precision.HIGHEST)
    mixed = jnp.einsum('tbj,jbc->tcj', inner, left_part, precision=lax.Precision.HIGHEST)
    return current + mixed.reshape(-1, D) * jax.nn.silu(normed)

def reference(tokens, gains, right_factors, left_factors):
    current = tokens
    for round_number in range(ROUNDS):
        for section in range(N_SEGMENT):
            current = one_layer(current, gains[section, round_number], right_factors[section, round_number], left_factors[section, round_number])
    return current
```

```python
import functools

import jax
import jax.numpy as jnp
from jax import lax
from jax.experimental import pallas as pl
from jax.experimental.pallas import tpu as pltpu
from jax.sharding import PartitionSpec as P

epsilon = 1e-06
exact = lax.Precision.HIGHEST
LANES = 128
ROWS = 8
PLANES = 4
QUARTERS = 4
CHUNKS = 2


def row_offset(step, mate, plane, quarter):
    start = ((plane + step) % PLANES) * (QUARTERS * ROWS) + (quarter ^ mate) * ROWS
    return pl.ds(pl.multiple_of(start, ROWS), ROWS)


def product(weight, value):
    return lax.dot_general(
        weight, value, (((0,), (0,)), ((), ())), precision=exact, preferred_element_type=jnp.float32
    )


def pick(parts, index, group):
    if len(parts) == 1:
        return parts[0][index]
    half = index // 4
    inside = index - half * 4
    return jnp.where(half == group, parts[0][inside], parts[1][inside])


def layer_edge_kernel(width, has_mix, has_next, place, *refs):
    refs = list(refs)

    def take(count):
        head = refs[:count]
        del refs[:count]
        return head

    plane, quarter, group = place[0], place[1], place[2]
    current = take(PLANES)
    if has_mix:
        old_gain = take(PLANES)
        squares_in = take(QUARTERS)
        mixed = [take(QUARTERS) for _ in range(CHUNKS)]
    if has_next:
        gain = take(PLANES)
        weights = [take(1 if step == 0 else 2) for step in range(PLANES)]
    fresh = take(PLANES) if has_mix else current
    if has_next:
        send = [take(QUARTERS) for _ in range(CHUNKS)]
        square_ref, tile = take(2)
        square_ref[...] = jnp.zeros_like(square_ref)
    per_chunk = PLANES // CHUNKS

    if has_mix:
        total = sum(ref[pl.ds(512, ROWS), :] for ref in squares_in)
        scale = lax.rsqrt(jnp.sum(total, axis=0, keepdims=True) / width + epsilon)
        for step in range(PLANES):

            @pl.loop(0, ROWS)
            def _(index, step=step):
                for other in range(PLANES):
                    for mate in range(QUARTERS):
                        where = row_offset(other, mate, plane, quarter)
                        value = current[step][index, where, :]
                        block = (other % per_chunk) * 32 + step * ROWS + index
                        start = pl.multiple_of(block * ROWS, ROWS)
                        mix = mixed[other // per_chunk][mate][pl.ds(start, ROWS), :]
                        normed = value * scale * old_gain[step][index, where, :]
                        value = value + (mix * scale) * (normed / (1.0 + jnp.exp(-normed)))
                        fresh[step][index, where, :] = value

    if has_next:
        for step in range(PLANES):

            @pl.loop(0, ROWS)
            def _(index, step=step):
                value = fresh[step][index]
                square_ref[...] += jnp.sum((value * value).reshape(16, ROWS, LANES), axis=0)
                weight = pick(weights[step], index, group)
                tile[index] = product(weight, value * gain[step][index])
                for other in range(PLANES):
                    for mate in range(QUARTERS):
                        block = (other % per_chunk) * 32 + step * ROWS + index
                        start = pl.multiple_of(block * ROWS, ROWS)
                        send[other // per_chunk][mate][pl.ds(start, ROWS), :] = tile[
                            index, row_offset(other, mate, plane, quarter), :
                        ]

        for mate in range(QUARTERS):
            send[0][mate][pl.ds(512, ROWS), :] = square_ref[...]


def column_kernel(chunk, place, *refs):
    refs = list(refs)

    def take(count):
        head = refs[:count]
        del refs[:count]
        return head

    plane, quarter, group = place[0], place[1], place[2]
    per_chunk = PLANES // CHUNKS
    came = take(QUARTERS)
    weights = [take(1 if chunk * per_chunk + n == 0 else 2) for n in range(per_chunk)]
    send = take(QUARTERS)
    value, tile = take(2)
    for n in range(per_chunk):

        @pl.loop(0, ROWS)
        def _(index, n=n):
            for step in range(PLANES):
                for mate in range(QUARTERS):
                    start = (n * 32 + step * ROWS) * ROWS + index
                    value[index, row_offset(step, mate, plane, quarter), :] = came[mate][
                        pl.ds(start, ROWS, stride=ROWS), :
                    ]
            tile[index] = product(pick(weights[n], index, group), value[index])
            for step in range(PLANES):
                for mate in range(QUARTERS):
                    start = (n * 32 + step * ROWS) * ROWS + index
                    send[mate][pl.ds(start, ROWS, stride=ROWS), :] = tile[
                        index, row_offset(step, mate, plane, quarter), :
                    ]


SMALL = pl.BlockSpec(memory_space=pltpu.SMEM)
WHOLE = pl.BlockSpec(memory_space=pltpu.VMEM)
PARAMS = pltpu.CompilerParams(vmem_limit_bytes=40 * 1024 * 1024)


def array(*shape):
    return jax.ShapeDtypeStruct(shape, jnp.float32)


def call(kernel, operands, outs, scratch, flops):
    moved = 4 * (sum(a.size for a in operands) + sum(o.size for o in outs))
    return pl.pallas_call(
        kernel,
        out_shape=outs,
        in_specs=[SMALL] + [WHOLE] * (len(operands) - 1),
        out_specs=[WHOLE] * len(outs),
        scratch_shapes=scratch,
        compiler_params=PARAMS,
        cost_estimate=pl.CostEstimate(flops=flops, bytes_accessed=moved, transcendentals=0),
    )(*operands)


PIECE = (ROWS, LANES, LANES)
STAGE_FLOPS = 2 * 32 * LANES * LANES * LANES


def layer_edge(width, place, current, mix=None, following=None):
    operands = [place, *current]
    outs, scratch = [], []
    if mix is not None:
        old_gain, squares, mixed = mix
        operands += [*old_gain, *squares, *mixed[0], *mixed[1]]
        outs += [array(*PIECE)] * PLANES
    if following is not None:
        gain, weights = following
        operands += [*gain, *(part for parts in weights for part in parts)]
        outs += [array(520, LANES)] * QUARTERS + [array(512, LANES)] * QUARTERS
        scratch = [pltpu.VMEM((ROWS, LANES), jnp.float32), pltpu.VMEM(PIECE, jnp.float32)]
    kernel = functools.partial(layer_edge_kernel, width, mix is not None, following is not None)
    results = list(call(kernel, operands, outs, scratch, 6 * STAGE_FLOPS))
    fresh = current
    if mix is not None:
        fresh, results = results[:PLANES], results[PLANES:]
    return fresh, [results[:QUARTERS], results[QUARTERS:]]


def column_stage(chunk, place, came, weights):
    operands = [place, *came, *(part for parts in weights for part in parts)]
    scratch = [pltpu.VMEM(PIECE, jnp.float32)] * 2
    outs = [array(512, LANES)] * QUARTERS
    return call(functools.partial(column_kernel, chunk), operands, outs, scratch, 3 * STAGE_FLOPS)


def routed(value, to):
    route = []
    for core in range(2):
        for z in range(PLANES):
            for y in range(2):
                there = to(core, z, y)
                route.append((core * 8 + z * 2 + y, there[0] * 8 + there[1] * 2 + there[2]))
    return lax.ppermute(value, ("segment", "block"), route)


def core_swap(value):
    return routed(value, lambda core, z, y: (1 - core, z, y))


def ring(value, distance):
    return routed(value, lambda core, z, y: (core, (z + distance) % PLANES, y))


def to_mate(value, mate):
    return routed(value, lambda core, z, y: (core ^ (mate & 1), z, y ^ (mate >> 1)))


def group_swap(value):
    return lax.ppermute(value, "groups", [(0, 1), (1, 0)])


def exchange(chunk):
    return [chunk[0]] + [to_mate(chunk[mate], mate) for mate in range(1, QUARTERS)]


def plane_body(tokens, gains, right_factors, left_factors):
    core = lax.axis_index("segment")
    block = lax.axis_index("block")
    group = lax.axis_index("groups")
    z, y = block // 2, block % 2
    place = jnp.stack([z, y * 2 + core, group]).astype(jnp.int32)
    rounds = right_factors.shape[1]
    layers = 2 * rounds
    width = right_factors.shape[3] * 8 * right_factors.shape[2]

    folded = tokens.reshape(2, LANES, 2, ROWS, LANES).transpose(2, 0, 3, 4, 1)
    mine = lax.dynamic_index_in_dim(folded, core, 0, keepdims=False)
    theirs = core_swap(lax.dynamic_index_in_dim(folded, 1 - core, 0, keepdims=False))
    four = jnp.stack([mine, theirs]).reshape((4,) + PIECE)
    current = []
    for step in range(PLANES):
        plane = (z - step) % PLANES
        slot = (plane // 2 ^ core) * 2 + plane % 2
        piece = lax.dynamic_index_in_dim(four, slot, 0, keepdims=False)
        current.append(piece if step == 0 else ring(piece, -step))

    mine = lax.dynamic_slice_in_dim(gains[0].reshape(rounds, 2 * ROWS, LANES), core * ROWS, ROWS, 1)
    theirs = core_swap(lax.dynamic_slice_in_dim(gains[0].reshape(rounds, 2 * ROWS, LANES), (1 - core) * ROWS, ROWS, 1))
    first = jnp.where(core == 0, mine, theirs)
    second = jnp.where(core == 0, theirs, mine)
    held = jnp.stack([first, second], axis=1).reshape(layers, ROWS, LANES)
    gain_pieces = []
    for step in range(PLANES):
        gain_pieces.append(held)
        if step < PLANES - 1:
            held = ring(held, -1)
    gain = [
        [jnp.broadcast_to(piece[layer][:, :, None], PIECE) for piece in gain_pieces] for layer in range(layers)
    ]

    def gathered(factors):
        found = [None] * layers
        for r in range(rounds):
            mine = lax.dynamic_slice_in_dim(factors[0, r], core * ROWS, ROWS, 0)
            theirs = core_swap(lax.dynamic_slice_in_dim(factors[0, r], (1 - core) * ROWS, ROWS, 0))
            found[2 * r] = jnp.where(core == 0, mine, theirs)
            found[2 * r + 1] = jnp.where(core == 0, theirs, mine)
        pieces = []
        for layer in range(layers):
            parts = [(found[layer],)]
            half = lax.dynamic_slice_in_dim(found[layer], group * 4, 4, 0)
            for _ in range(PLANES - 1):
                half = ring(half, -1)
                parts.append((half, group_swap(half)))
            pieces.append(parts)
        return pieces

    right = gathered(right_factors)
    left = gathered(left_factors)

    _, sends = layer_edge(width, place, current, None, (gain[0], right[0]))
    for layer in range(layers):
        came = [exchange(sends[0]), exchange(sends[1])]
        mixed = []
        for chunk in range(CHUNKS):
            weights = left[layer][chunk * 2 : chunk * 2 + 2]
            mixed.append(exchange(column_stage(chunk, place, came[chunk], weights)))
        following = (gain[layer + 1], right[layer + 1]) if layer + 1 < layers else None
        current, sends = layer_edge(width, place, current, (gain[layer], came[0], mixed), following)

    back = [None] * PLANES
    for step in range(PLANES):
        back[step] = current[step] if step == 0 else ring(current[step], step)
    stacked = jnp.stack(back)
    ordered = jnp.stack([lax.dynamic_index_in_dim(stacked, (z - p) % PLANES, 0, keepdims=False) for p in range(PLANES)])
    ordered = ordered.reshape((2, 2) + PIECE)
    mine = lax.dynamic_index_in_dim(ordered, core, 0, keepdims=False)
    theirs = core_swap(lax.dynamic_index_in_dim(ordered, 1 - core, 0, keepdims=False))
    both = jnp.stack([jnp.where(core == 0, mine, theirs), jnp.where(core == 0, theirs, mine)])
    return both.transpose(1, 4, 0, 2, 3).reshape(tokens.shape)


def wide_body(tokens, gains, right_factors, left_factors):
    blocks_here, block_size = right_factors.shape[2:4]
    token_count, width_here = tokens.shape
    width = width_here * lax.axis_size("block")
    rounds = right_factors.shape[1]
    core = lax.axis_index("segment")
    count = lax.axis_size("segment")

    def gathered(value):
        return lax.all_gather(value[0], "segment", axis=0)

    gains, right_factors, left_factors = gathered(gains), gathered(right_factors), gathered(left_factors)
    current = tokens.T
    for layer in range(count * rounds):
        s, r = layer % count, layer // count
        sum_squares = lax.psum(jnp.sum(current * current, axis=0), "block")
        normed = current * lax.rsqrt(sum_squares / width + epsilon)[None, :] * gains[s, r][:, None]
        inner = jnp.einsum(
            "bit,bij->bjt",
            normed.reshape(blocks_here, block_size, token_count),
            right_factors[s, r],
            precision=exact,
        )
        combined = jnp.einsum(
            "bjt,jbc->cjt",
            lax.all_to_all(inner, "block", split_axis=1, concat_axis=0, tiled=True),
            left_factors[s, r],
            precision=exact,
        )
        mixed = lax.all_to_all(combined, "block", split_axis=0, concat_axis=1, tiled=True)
        current = current + mixed.reshape(width_here, token_count) * jax.nn.silu(normed)
    return current.T


def solution(mesh):
    placed = (
        P(("groups", "segment"), "block"),
        P("segment", None, "block"),
        P("segment", None, "block", None, None),
        P("segment", None, "block", None, None),
    )
    planes = dict(mesh.shape) == {"groups": 2, "segment": 2, "block": 8}

    def body(tokens, gains, right_factors, left_factors):
        fits = planes and tokens.shape == (256, 2048) and right_factors.shape[2:] == (16, 128, 128)
        return (plane_body if fits else wide_body)(tokens, gains, right_factors, left_factors)

    return jax.shard_map(
        body,
        mesh=mesh,
        in_specs=placed,
        out_specs=P(("groups", "segment"), "block"),
        check_vma=False,
    )
```

```python
import functools

import jax
import jax.numpy as jnp
from jax import lax
from jax.experimental import pallas as pl
from jax.experimental.pallas import tpu as pltpu
from jax.sharding import PartitionSpec as P

epsilon = 1e-06
exact = lax.Precision.HIGHEST
LANES = 128
ROWS = 8
PLANES = 4
QUARTERS = 4
CHUNKS = 2


def gray(position):
    return position ^ (position >> 1)


def row_offset(step, mate, position, quarter):
    start = gray((position + step) % PLANES) * (QUARTERS * ROWS) + (quarter ^ mate) * ROWS
    return pl.ds(pl.multiple_of(start, ROWS), ROWS)


def halves(value):
    high = value.astype(jnp.bfloat16)
    return high, (value - high.astype(jnp.float32)).astype(jnp.bfloat16)


def product(weight, value):
    def dot(a, b):
        return lax.dot_general(a, b, (((0,), (0,)), ((), ())), preferred_element_type=jnp.float32)

    weight_high, weight_low = halves(weight)
    value_high, value_low = halves(value)
    return dot(weight_high, value_high) + (dot(weight_high, value_low) + dot(weight_low, value_high))


def pick(parts, index, group):
    if len(parts) == 1:
        return parts[0][index]
    inside = parts[2] + index % 4
    if index < 4:
        return jnp.where(group == 0, parts[0][inside], parts[1][inside])
    return jnp.where(group == 0, parts[1][inside], parts[0][inside])


def sent_tile(step, index, other, by_piece):
    if by_piece:
        return step, (other * ROWS + index) * ROWS
    return other // 2, ((other % 2) * 32 + step * ROWS + index) * ROWS


class Taker:
    def __init__(self, refs):
        self.refs = list(refs)

    def __call__(self, count):
        head, self.refs = self.refs[:count], self.refs[count:]
        return head


def read_place(place):
    return place[0], place[1], place[2]


def take_weights(take, bases):
    return [take(1) if base is None else take(2) + [base] for base in bases]


def first_factor(steps, by_piece, current, gain, weights, send, tile, place):
    position, quarter, group = place
    squares = jnp.zeros((ROWS, LANES), jnp.float32)
    for n, step in enumerate(steps):
        for index in range(ROWS):
            value = current[n][index]
            squares += jnp.sum((value * value).reshape(LANES // ROWS, ROWS, LANES), axis=0)
            tile[index] = product(pick(weights[n], index, group), value * gain[n][index])
        for index in range(ROWS):
            for other in range(PLANES):
                for mate in range(QUARTERS):
                    part, start = sent_tile(step, index, other, by_piece)
                    ref = send[0 if by_piece else part][mate]
                    ref[pl.ds(start, ROWS), :] = tile[index, row_offset(other, mate, position, quarter), :]
    for ref in send[0]:
        ref[pl.ds(ref.shape[0] - ROWS, ROWS), :] = squares


def first_kernel(step, bases, place, *refs):
    take = Taker(refs)
    current, gain = take(1), take(1)
    weights = take_weights(take, bases)
    send, tile = [take(QUARTERS)], take(1)[0]
    first_factor([step], True, current, gain, weights, send, tile, read_place(place))


def edge_kernel(width, squares_count, has_next, bases, place, *refs):
    take = Taker(refs)
    position, quarter, group = read_place(place)
    current, old_gain = take(PLANES), take(PLANES)
    squares_in = take(squares_count)
    mixed = [take(QUARTERS) for _ in range(CHUNKS)]
    if has_next:
        gain = take(PLANES)
        weights = take_weights(take, bases)
    fresh = take(PLANES)
    if has_next:
        send, tile = [take(QUARTERS) for _ in range(CHUNKS)], take(1)[0]

    total = sum(ref[pl.ds(ref.shape[0] - ROWS, ROWS), :] for ref in squares_in)
    scale = lax.rsqrt(jnp.sum(total, axis=0, keepdims=True) / width + epsilon)
    scale = jnp.broadcast_to(scale, (ROWS, LANES))
    for step in range(PLANES):

        def finish(index, carry, step=step):
            for other in range(PLANES):
                for mate in range(QUARTERS):
                    where = row_offset(other, mate, position, quarter)
                    value = current[step][index, where, :]
                    part, start = sent_tile(step, index, other, False)
                    mix = mixed[part][mate][pl.ds(pl.multiple_of(start, ROWS), ROWS), :]
                    normed = value * scale * old_gain[step][index, where, :]
                    value = value + (mix * scale) * (normed / (1.0 + jnp.exp(-normed)))
                    fresh[step][index, where, :] = value
            return carry

        lax.fori_loop(0, ROWS, finish, 0, unroll=2)

    if has_next:
        first_factor(range(PLANES), False, fresh, gain, weights, send, tile, (position, quarter, group))


def column_kernel(chunk, by_piece, bases, has_gain, place, *refs):
    take = Taker(refs)
    position, quarter, group = read_place(place)
    came = [take(QUARTERS) for _ in range(PLANES if by_piece else 1)]
    weights = take_weights(take, bases)
    rows = take(PLANES) if has_gain else []
    send = take(QUARTERS)
    spread = take(PLANES) if has_gain else []
    value, tile = take(2)
    for n in range(2):
        other = chunk * 2 + n
        for index in range(ROWS):
            for step in range(PLANES):
                for mate in range(QUARTERS):
                    part, start = sent_tile(step, 0, other, by_piece)
                    ref = came[part if by_piece else 0][mate]
                    value[index, row_offset(step, mate, position, quarter), :] = ref[
                        pl.ds(start + index, ROWS, stride=ROWS), :
                    ]
            tile[index] = product(pick(weights[n], index, group), value[index])
            for step in range(PLANES):
                for mate in range(QUARTERS):
                    _, start = sent_tile(step, 0, other, False)
                    send[mate][pl.ds(start + index, ROWS, stride=ROWS), :] = tile[
                        index, row_offset(step, mate, position, quarter), :
                    ]
    for step in range(len(rows)):
        columns = rows[step][...].T
        for index in range(ROWS):
            spread[step][index] = jnp.broadcast_to(columns[:, index : index + 1], (LANES, LANES))


SMALL = pl.BlockSpec(memory_space=pltpu.SMEM)
WHOLE = pl.BlockSpec(memory_space=pltpu.VMEM)
PARAMS = pltpu.CompilerParams(vmem_limit_bytes=40 * 1024 * 1024)
PIECE = (ROWS, LANES, LANES)


def array(*shape):
    return jax.ShapeDtypeStruct(shape, jnp.float32)


def call(kernel, operands, outs, scratch, flops):
    moved = 4 * (sum(a.size for a in operands) + sum(o.size for o in outs))
    return pl.pallas_call(
        kernel,
        out_shape=outs,
        in_specs=[SMALL] + [WHOLE] * (len(operands) - 1),
        out_specs=[WHOLE] * len(outs),
        scratch_shapes=[pltpu.VMEM(PIECE, jnp.float32)] * scratch,
        compiler_params=PARAMS,
        cost_estimate=pl.CostEstimate(flops=flops, bytes_accessed=moved, transcendentals=0),
    )(*operands)


STAGE_FLOPS = 6 * 32 * LANES * LANES * LANES


def split_weights(weights):
    return [part for parts in weights for part in parts[:2]], [None if len(p) == 1 else p[2] for p in weights]


def first_piece(step, place, current, gain, weights):
    operands, bases = split_weights([weights])
    kernel = functools.partial(first_kernel, step, bases)
    return call(kernel, [place, current, gain, *operands], [array(264, LANES)] * QUARTERS, 1, STAGE_FLOPS // 4)


def layer_edge(width, place, current, old_gain, squares, mixed, following=None):
    operands = [place, *current, *old_gain, *squares, *mixed[0], *mixed[1]]
    outs, bases = [array(*PIECE)] * PLANES, None
    if following is not None:
        gain, weights = following
        more, bases = split_weights(weights)
        operands += [*gain, *more]
        outs += [array(520, LANES)] * QUARTERS + [array(512, LANES)] * QUARTERS
    kernel = functools.partial(edge_kernel, width, len(squares), following is not None, bases)
    results = list(call(kernel, operands, outs, int(following is not None), 2 * STAGE_FLOPS))
    return results[:PLANES], [results[PLANES : PLANES + QUARTERS], results[PLANES + QUARTERS :]]


def column_stage(chunk, by_piece, place, came, weights, rows=()):
    more, bases = split_weights(weights)
    operands = [place, *(ref for part in came for ref in part), *more, *rows]
    outs = [array(512, LANES)] * QUARTERS + [array(*PIECE)] * len(rows)
    kernel = functools.partial(column_kernel, chunk, by_piece, bases, bool(rows))
    results = list(call(kernel, operands, outs, 2, STAGE_FLOPS))
    return results[:QUARTERS], results[QUARTERS:]


def routed(value, to):
    route = []
    for core in range(2):
        for z in range(PLANES):
            for y in range(2):
                there = to(core, z, y)
                route.append((core * 8 + z * 2 + y, there[0] * 8 + there[1] * 2 + there[2]))
    return lax.ppermute(value, ("segment", "block"), route)


def core_swap(value):
    return routed(value, lambda core, z, y: (1 - core, z, y))


def ring(value, distance):
    return routed(value, lambda core, z, y: (core, gray((gray(z) + distance) % PLANES), y))


def to_mate(value, mate):
    return routed(value, lambda core, z, y: (core ^ (mate & 1), z, y ^ (mate >> 1)))


def group_swap(value):
    return lax.ppermute(value, "groups", [(0, 1), (1, 0)])


def exchange(chunk):
    return [chunk[0]] + [to_mate(chunk[mate], mate) for mate in range(1, QUARTERS)]


def after(value, *earlier):
    return lax.optimization_barrier((value, *earlier))[0]


def plane_body(tokens, gains, right_factors, left_factors):
    core = lax.axis_index("segment")
    block = lax.axis_index("block")
    group = lax.axis_index("groups")
    z, y = block // 2, block % 2
    position = gray(z)
    place = jnp.stack([position, y * 2 + core, group]).astype(jnp.int32)
    rounds = right_factors.shape[1]
    layers = 2 * rounds
    width = right_factors.shape[3] * 8 * right_factors.shape[2]

    def swapped(value):
        mine = lax.dynamic_slice_in_dim(value, core * ROWS, ROWS, 0)
        theirs = core_swap(lax.dynamic_slice_in_dim(value, (1 - core) * ROWS, ROWS, 0))
        return jnp.where(core == 0, mine, theirs), jnp.where(core == 0, theirs, mine)

    folded = tokens.reshape(2, LANES, 2, ROWS, LANES).transpose(2, 0, 3, 4, 1)
    mine = lax.dynamic_index_in_dim(folded, core, 0, keepdims=False)
    theirs = core_swap(lax.dynamic_index_in_dim(folded, 1 - core, 0, keepdims=False))
    four = jnp.stack([mine, theirs]).reshape((4,) + PIECE)
    current = []
    for step in range(PLANES):
        plane = gray((position - step) % PLANES)
        slot = ((plane // 2) ^ core) * 2 + plane % 2
        piece = lax.dynamic_index_in_dim(four, slot, 0, keepdims=False)
        current.append(piece if step == 0 else ring(piece, -step))

    held = jnp.moveaxis(gains[0].reshape(rounds, 2 * ROWS, LANES), 1, 0)
    held = jnp.stack(swapped(held), axis=2).transpose(1, 2, 0, 3).reshape(layers, ROWS, LANES)
    gain_pieces = [held]
    for _ in range(PLANES - 1):
        held = ring(held, -1)
        gain_pieces.append(held)
    gain_rows = [[piece[layer] for piece in gain_pieces] for layer in range(layers)]

    right, left = [None] * layers, [None] * layers
    for r in range(rounds):
        right[2 * r], right[2 * r + 1] = swapped(right_factors[0, r])
        left[2 * r], left[2 * r + 1] = swapped(left_factors[0, r])

    def my_half(value):
        return lax.dynamic_slice_in_dim(value, group * 4, 4, 0)

    def chain(half):
        found = []
        for _ in range(PLANES - 1):
            half = ring(half, -1)
            found.append((half, group_swap(half)))
        return found

    right_parts, left_parts = [], []
    right_chain = chain(my_half(right[0]))
    left_chain = chain(after(my_half(left[0]), right_chain[-1][0]))
    right_parts.append([(right[0],)] + [(*pair, 0) for pair in right_chain])
    left_parts.append([(left[0],)] + [(*pair, 0) for pair in left_chain])
    last = left_chain[-1][0]
    for layer in range(1, layers):
        both = jnp.concatenate([my_half(right[layer]), my_half(left[layer])])
        both_chain = chain(after(both, last))
        last = both_chain[-1][0]
        right_parts.append([(right[layer],)] + [(*pair, 0) for pair in both_chain])
        left_parts.append([(left[layer],)] + [(*pair, 4) for pair in both_chain])

    gain = [jnp.broadcast_to(row[:, :, None], PIECE) for row in gain_rows[0]]
    came = [
        exchange(first_piece(step, place, current[step], gain[step], right_parts[0][step])) for step in range(PLANES)
    ]
    for layer in range(layers):
        by_piece = layer == 0
        squares = [part[mate] for part in (came if by_piece else came[:1]) for mate in range(QUARTERS)]
        mixed, next_gain = [], None
        for chunk in range(CHUNKS):
            rows = gain_rows[layer + 1] if chunk == 0 and layer + 1 < layers else ()
            weights = left_parts[layer][chunk * 2 : chunk * 2 + 2]
            source = came if by_piece else came[chunk : chunk + 1]
            sends, spread = column_stage(chunk, by_piece, place, source, weights, rows)
            mixed.append(exchange(sends))
            next_gain = spread or next_gain
        following = (next_gain, right_parts[layer + 1]) if layer + 1 < layers else None
        current, sends = layer_edge(width, place, current, gain, squares, mixed, following)
        gain = next_gain
        if following is not None:
            came = [exchange(sends[0]), exchange(sends[1])]

    back = [current[step] if step == 0 else ring(current[step], step) for step in range(PLANES)]
    stacked = jnp.stack(back)
    ordered = jnp.stack(
        [
            lax.dynamic_index_in_dim(stacked, (position - gray(plane)) % PLANES, 0, keepdims=False)
            for plane in range(PLANES)
        ]
    ).reshape((2, 2) + PIECE)
    mine = lax.dynamic_index_in_dim(ordered, core, 0, keepdims=False)
    theirs = core_swap(lax.dynamic_index_in_dim(ordered, 1 - core, 0, keepdims=False))
    both = jnp.stack([jnp.where(core == 0, mine, theirs), jnp.where(core == 0, theirs, mine)])
    return both.transpose(1, 4, 0, 2, 3).reshape(tokens.shape)


def wide_body(tokens, gains, right_factors, left_factors):
    blocks_here, block_size = right_factors.shape[2:4]
    token_count, width_here = tokens.shape
    width = width_here * lax.axis_size("block")
    rounds = right_factors.shape[1]
    core = lax.axis_index("segment")
    count = lax.axis_size("segment")

    def gathered(value):
        return lax.all_gather(value[0], "segment", axis=0)

    gains, right_factors, left_factors = gathered(gains), gathered(right_factors), gathered(left_factors)
    current = tokens.T
    for layer in range(count * rounds):
        s, r = layer % count, layer // count
        sum_squares = lax.psum(jnp.sum(current * current, axis=0), "block")
        normed = current * lax.rsqrt(sum_squares / width + epsilon)[None, :] * gains[s, r][:, None]
        inner = jnp.einsum(
            "bit,bij->bjt",
            normed.reshape(blocks_here, block_size, token_count),
            right_factors[s, r],
            precision=exact,
        )
        combined = jnp.einsum(
            "bjt,jbc->cjt",
            lax.all_to_all(inner, "block", split_axis=1, concat_axis=0, tiled=True),
            left_factors[s, r],
            precision=exact,
        )
        mixed = lax.all_to_all(combined, "block", split_axis=0, concat_axis=1, tiled=True)
        current = current + mixed.reshape(width_here, token_count) * jax.nn.silu(normed)
    return current.T


def solution(mesh):
    placed = (
        P(("groups", "segment"), "block"),
        P("segment", None, "block"),
        P("segment", None, "block", None, None),
        P("segment", None, "block", None, None),
    )
    planes = dict(mesh.shape) == {"groups": 2, "segment": 2, "block": 8}

    def body(tokens, gains, right_factors, left_factors):
        fits = planes and tokens.shape == (256, 2048) and right_factors.shape[2:] == (16, 128, 128)
        return (plane_body if fits else wide_body)(tokens, gains, right_factors, left_factors)

    return jax.shard_map(
        body,
        mesh=mesh,
        in_specs=placed,
        out_specs=P(("groups", "segment"), "block"),
        check_vma=False,
    )
```

```python
import functools

import jax
import jax.numpy as jnp
from jax import lax
from jax.experimental import pallas as pl
from jax.experimental.pallas import tpu as pltpu
from jax.sharding import PartitionSpec as P

epsilon = 1e-06
exact = lax.Precision.HIGHEST
LANES = 128
ROWS = 8
PLANES = 4
QUARTERS = 4
CHUNKS = 2


def gray(position):
    return position ^ (position >> 1)


def row_offset(step, mate, position, quarter):
    start = gray((position + step) % PLANES) * (QUARTERS * ROWS) + (quarter ^ mate) * ROWS
    return pl.ds(pl.multiple_of(start, ROWS), ROWS)


def halves(value):
    high = value.astype(jnp.bfloat16)
    return high, (value - high.astype(jnp.float32)).astype(jnp.bfloat16)


def product(weight, value):
    def dot(a, b):
        return lax.dot_general(a, b, (((0,), (0,)), ((), ())), preferred_element_type=jnp.float32)

    weight_high, weight_low = halves(weight)
    value_high, value_low = halves(value)
    return dot(weight_high, value_high) + (dot(weight_high, value_low) + dot(weight_low, value_high))


def pick(piece, index, group):
    kind, base, refs = piece
    if kind == "whole":
        return refs[0][base + index]
    if kind == "halves":
        inside = base + index % 4
        owner = index // 4
    else:
        inside = base + index
        owner = 0 if kind == "next" else 1
    return jnp.where(group == owner, refs[0][inside], refs[1][inside])


def sent_tile(step, index, other, by_piece):
    if by_piece:
        return step, (other * ROWS + index) * ROWS
    return other // 2, ((other % 2) * 32 + step * ROWS + index) * ROWS


class Taker:
    def __init__(self, refs):
        self.refs = list(refs)

    def __call__(self, count):
        head, self.refs = self.refs[:count], self.refs[count:]
        return head


def read_place(place):
    return place[0], place[1], place[2]


def take_weights(take, kinds):
    return [(kind, base, take(1 if kind == "whole" else 2)) for kind, base in kinds]


def first_factor(steps, by_piece, current, gain, weights, send, tile, place):
    position, quarter, group = place
    squares = jnp.zeros((ROWS, LANES), jnp.float32)
    for n, step in enumerate(steps):
        for index in range(ROWS):
            value = current[n][index]
            squares += jnp.sum((value * value).reshape(LANES // ROWS, ROWS, LANES), axis=0)
            tile[index] = product(pick(weights[n], index, group), value * gain[n][index])
        for index in range(ROWS):
            for other in range(PLANES):
                for mate in range(QUARTERS):
                    part, start = sent_tile(step, index, other, by_piece)
                    ref = send[0 if by_piece else part][mate]
                    ref[pl.ds(start, ROWS), :] = tile[index, row_offset(other, mate, position, quarter), :]
    for ref in send[0]:
        ref[pl.ds(ref.shape[0] - ROWS, ROWS), :] = squares


def first_kernel(step, kinds, place, *refs):
    take = Taker(refs)
    tokens, gain = take(1)[0], take(1)
    weights = take_weights(take, kinds)
    current, send, tile = take(1), [take(QUARTERS)], take(1)[0]
    for index in range(ROWS):
        current[0][index] = tokens[:, pl.ds(index * LANES, LANES)].T
    first_factor([step], True, current, gain, weights, send, tile, read_place(place))


def last_kernel(width, step, squares_count, place, *refs):
    take = Taker(refs)
    position, quarter, _ = read_place(place)
    current, old_gain, squares_in, mixed = take(1)[0], take(1)[0], take(squares_count), take(QUARTERS)
    result, tile = take(2)
    scale = token_scale(width, squares_in)
    for index in range(ROWS):
        for other in range(PLANES):
            for mate in range(QUARTERS):
                where = row_offset(other, mate, position, quarter)
                _, start = sent_tile(step, index, other, True)
                mix = mixed[mate][pl.ds(start, ROWS), :]
                tile[index, where, :] = residual(current[index, where, :], mix, scale, old_gain[index, where, :])
        result[:, pl.ds(index * LANES, LANES)] = tile[index].T


def token_scale(width, squares):
    total = sum(ref[pl.ds(ref.shape[0] - ROWS, ROWS), :] for ref in squares)
    scale = lax.rsqrt(jnp.sum(total, axis=0, keepdims=True) / width + epsilon)
    return jnp.broadcast_to(scale, (ROWS, LANES))


def residual(value, mix, scale, gain):
    normed = value * scale * gain
    return value + (mix * scale) * (normed / (1.0 + jnp.exp(-normed)))


def edge_kernel(width, squares_count, kinds, place, *refs):
    take = Taker(refs)
    position, quarter, group = read_place(place)
    current, old_gain = take(PLANES), take(PLANES)
    squares_in = take(squares_count)
    mixed = [take(QUARTERS) for _ in range(CHUNKS)]
    gain = take(PLANES)
    weights = take_weights(take, kinds)
    fresh = take(PLANES)
    send, tile = [take(QUARTERS) for _ in range(CHUNKS)], take(1)[0]
    scale = token_scale(width, squares_in)
    for step in range(PLANES):

        def finish(index, carry, step=step):
            for other in range(PLANES):
                for mate in range(QUARTERS):
                    where = row_offset(other, mate, position, quarter)
                    value = current[step][index, where, :]
                    part, start = sent_tile(step, index, other, False)
                    mix = mixed[part][mate][pl.ds(pl.multiple_of(start, ROWS), ROWS), :]
                    gained = old_gain[step][index, where, :]
                    fresh[step][index, where, :] = residual(value, mix, scale, gained)
            return carry

        lax.fori_loop(0, ROWS, finish, 0, unroll=2)

    first_factor(range(PLANES), False, fresh, gain, weights, send, tile, (position, quarter, group))


def column_kernel(others, in_pieces, out_pieces, kinds, has_gain, place, *refs):
    take = Taker(refs)
    position, quarter, group = read_place(place)
    came = [take(QUARTERS) for _ in range(PLANES if in_pieces else len(others) // 2)]
    weights = take_weights(take, kinds)
    rows = take(PLANES) if has_gain else []
    send = [take(QUARTERS) for _ in range(PLANES if out_pieces else len(others) // 2)]
    spread = take(PLANES) if has_gain else []
    value, tile = take(2)
    for n, other in enumerate(others):
        for index in range(ROWS):
            for step in range(PLANES):
                for mate in range(QUARTERS):
                    part, start = sent_tile(step, 0, other, in_pieces)
                    ref = came[part if in_pieces else n // 2][mate]
                    value[index, row_offset(step, mate, position, quarter), :] = ref[
                        pl.ds(start + index, ROWS, stride=ROWS), :
                    ]
            tile[index] = product(pick(weights[n], index, group), value[index])
            for step in range(PLANES):
                for mate in range(QUARTERS):
                    part, start = sent_tile(step, 0, other, out_pieces)
                    send[part if out_pieces else n // 2][mate][pl.ds(start + index, ROWS, stride=ROWS), :] = tile[
                        index, row_offset(step, mate, position, quarter), :
                    ]
    for step in range(len(rows)):
        columns = rows[step][...].T
        for index in range(ROWS):
            spread[step][index] = jnp.broadcast_to(columns[:, index : index + 1], (LANES, LANES))


SMALL = pl.BlockSpec(memory_space=pltpu.SMEM)
WHOLE = pl.BlockSpec(memory_space=pltpu.VMEM)
PARAMS = pltpu.CompilerParams(vmem_limit_bytes=40 * 1024 * 1024)
PIECE = (ROWS, LANES, LANES)


def array(*shape):
    return jax.ShapeDtypeStruct(shape, jnp.float32)


def call(kernel, operands, outs, scratch, flops):
    moved = 4 * (sum(a.size for a in operands) + sum(o.size for o in outs))
    return pl.pallas_call(
        kernel,
        out_shape=outs,
        in_specs=[SMALL] + [WHOLE] * (len(operands) - 1),
        out_specs=[WHOLE] * len(outs),
        scratch_shapes=[pltpu.VMEM(PIECE, jnp.float32)] * scratch,
        compiler_params=PARAMS,
        cost_estimate=pl.CostEstimate(flops=flops, bytes_accessed=moved, transcendentals=0),
    )(*operands)


STAGE_FLOPS = 6 * 32 * LANES * LANES * LANES


def split_weights(weights):
    return [array for piece in weights for array in piece[2]], [piece[:2] for piece in weights]


def first_piece(step, place, tokens, gain, weights):
    operands, kinds = split_weights([weights])
    kernel = functools.partial(first_kernel, step, kinds)
    outs = [array(*PIECE)] + [array(264, LANES)] * QUARTERS
    results = list(call(kernel, [place, tokens, gain, *operands], outs, 1, STAGE_FLOPS // 4))
    return results[0], results[1:]


def last_piece(width, step, place, current, old_gain, squares, mixed):
    kernel = functools.partial(last_kernel, width, step, len(squares))
    operands = [place, current, old_gain, *squares, *mixed]
    return call(kernel, operands, [array(LANES, ROWS * LANES)], 1, STAGE_FLOPS // 4)[0]


def layer_edge(width, place, current, old_gain, squares, mixed, gain, weights):
    more, kinds = split_weights(weights)
    operands = [place, *current, *old_gain, *squares, *mixed[0], *mixed[1], *gain, *more]
    outs = [array(*PIECE)] * PLANES + [array(520, LANES)] * QUARTERS + [array(512, LANES)] * QUARTERS
    kernel = functools.partial(edge_kernel, width, len(squares), kinds)
    results = list(call(kernel, operands, outs, 1, 2 * STAGE_FLOPS))
    return results[:PLANES], [results[PLANES : PLANES + QUARTERS], results[PLANES + QUARTERS :]]


def column_stage(others, in_pieces, out_pieces, place, came, weights, rows=()):
    more, kinds = split_weights(weights)
    operands = [place, *(ref for part in came for ref in part), *more, *rows]
    outs = [array(256, LANES)] * (QUARTERS * PLANES) if out_pieces else [array(512, LANES)] * QUARTERS
    count = len(outs)
    outs = outs + [array(*PIECE)] * len(rows)
    kernel = functools.partial(column_kernel, others, in_pieces, out_pieces, kinds, bool(rows))
    results = list(call(kernel, operands, outs, 2, STAGE_FLOPS))
    return [results[n : n + QUARTERS] for n in range(0, count, QUARTERS)], results[count:]


def routed(value, to):
    route = []
    for core in range(2):
        for z in range(PLANES):
            for y in range(2):
                there = to(core, z, y)
                route.append((core * 8 + z * 2 + y, there[0] * 8 + there[1] * 2 + there[2]))
    return lax.ppermute(value, ("segment", "block"), route)


def core_swap(value):
    return routed(value, lambda core, z, y: (1 - core, z, y))


def ring(value, distance):
    return routed(value, lambda core, z, y: (core, gray((gray(z) + distance) % PLANES), y))


def group_ring(value):
    route = []
    for group in range(2):
        for core in range(2):
            for z in range(PLANES):
                for y in range(2):
                    there = gray((gray(z) + (1 if group else -1)) % PLANES)
                    start = group * 16 + core * 8 + y
                    route.append((start + z * 2, start + there * 2))
    return lax.ppermute(value, ("groups", "segment", "block"), route)


def to_mate(value, mate):
    return routed(value, lambda core, z, y: (core ^ (mate & 1), z, y ^ (mate >> 1)))


def group_swap(value):
    return lax.ppermute(value, "groups", [(0, 1), (1, 0)])


def exchange(chunk):
    return [chunk[0]] + [to_mate(chunk[mate], mate) for mate in range(1, QUARTERS)]


def after(value, *earlier):
    return lax.optimization_barrier((value, *earlier))[0]


def plane_body(tokens, gains, right_factors, left_factors):
    core = lax.axis_index("segment")
    block = lax.axis_index("block")
    group = lax.axis_index("groups")
    z, y = block // 2, block % 2
    position = gray(z)
    place = jnp.stack([position, y * 2 + core, group]).astype(jnp.int32)
    rounds = right_factors.shape[1]
    layers = 2 * rounds
    width = right_factors.shape[3] * 8 * right_factors.shape[2]

    def swapped(value):
        mine = lax.dynamic_slice_in_dim(value, core * ROWS, ROWS, 0)
        theirs = core_swap(lax.dynamic_slice_in_dim(value, (1 - core) * ROWS, ROWS, 0))
        return jnp.where(core == 0, mine, theirs), jnp.where(core == 0, theirs, mine)

    half = tokens.shape[1] // 2
    mine = lax.dynamic_slice_in_dim(tokens, core * half, half, 1)
    theirs = core_swap(lax.dynamic_slice_in_dim(tokens, (1 - core) * half, half, 1))
    pieces = []
    for step in range(PLANES):
        plane = gray((position - step) % PLANES)
        start = (plane % 2) * LANES
        kept = lax.dynamic_slice_in_dim(mine, start, LANES, 0)
        other = lax.dynamic_slice_in_dim(theirs, start, LANES, 0)
        pieces.append(jnp.where(plane // 2 == core, kept, other))
    arrived = [piece if step == 0 else ring(piece, -step) for step, piece in enumerate(pieces)]

    held = jnp.moveaxis(gains[0].reshape(rounds, 2 * ROWS, LANES), 1, 0)
    held = jnp.stack(swapped(held), axis=2).transpose(1, 2, 0, 3).reshape(layers, ROWS, LANES)
    gain_pieces = [held]
    for _ in range(PLANES - 1):
        held = ring(held, -1)
        gain_pieces.append(held)
    gain_rows = [[piece[layer] for piece in gain_pieces] for layer in range(layers)]

    right, left = [None] * layers, [None] * layers
    for r in range(rounds):
        right[2 * r], right[2 * r + 1] = swapped(right_factors[0, r])
        left[2 * r], left[2 * r + 1] = swapped(left_factors[0, r])

    def fetched(parts, earlier):
        together = parts[0] if len(parts) == 1 else jnp.concatenate(parts)
        near = group_ring(after(together, *earlier))
        folded = near.reshape(len(parts), 2, 4, LANES, LANES)
        far = group_ring(lax.dynamic_index_in_dim(folded, group, 1, keepdims=False).reshape(-1, LANES, LANES))
        near_pair, far_pair = (near, group_swap(near)), (far, group_swap(far))
        found = []
        for n, part in enumerate(parts):
            found.append(
                [
                    ("whole", 0, (part,)),
                    ("next", n * ROWS, near_pair),
                    ("halves", n * 4, far_pair),
                    ("previous", n * ROWS, near_pair),
                ]
            )
        return found, far

    right_parts, left_parts = [], []
    (found,), last = fetched([right[0]], [pieces[1]])
    right_parts.append(found)
    (found,), last = fetched([left[0]], [last])
    left_parts.append(found)
    for layer in range(1, layers):
        (found, more), last = fetched([right[layer], left[layer]], [last])
        right_parts.append(found)
        left_parts.append(more)

    gain = [jnp.broadcast_to(row[:, :, None], PIECE) for row in gain_rows[0]]
    current, came = [], []
    for step in range(PLANES):
        turned, sends = first_piece(step, place, arrived[step], gain[step], right_parts[0][step])
        current.append(turned)
        came.append(exchange(sends))
    for layer in range(layers - 1):
        in_pieces = layer == 0
        squares = [part[mate] for part in (came if in_pieces else came[:1]) for mate in range(QUARTERS)]
        mixed = []
        for chunk in range(CHUNKS):
            others = (chunk * 2, chunk * 2 + 1)
            rows = gain_rows[layer + 1] if chunk == 0 else ()
            weights = left_parts[layer][others[0] : others[1] + 1]
            source = came if in_pieces else came[chunk : chunk + 1]
            (sends,), spread = column_stage(others, in_pieces, False, place, source, weights, rows)
            mixed.append(exchange(sends))
            next_gain = spread or next_gain
        current, sends = layer_edge(
            width, place, current, gain, squares, mixed, next_gain, right_parts[layer + 1]
        )
        gain = next_gain
        came = [exchange(sends[0]), exchange(sends[1])]

    squares = came[0]
    sends, _ = column_stage(tuple(range(PLANES)), False, True, place, came, left_parts[-1])
    back = [None] * PLANES
    for step in (2, 1, 3, 0):
        mixed = exchange(sends[step])
        done = last_piece(width, step, place, current[step], gain[step], squares, mixed)
        back[step] = done if step == 0 else ring(done, step)
    stacked = jnp.stack(back)

    def found_for(half_index):
        planes = [half_index * 2 + n for n in range(2)]
        return jnp.stack(
            [lax.dynamic_index_in_dim(stacked, (position - gray(p)) % PLANES, 0, keepdims=False) for p in planes]
        ).reshape(tokens.shape[0], half)

    mine = found_for(core)
    theirs = core_swap(found_for(1 - core))
    return jnp.where(core == 0, jnp.concatenate([mine, theirs], 1), jnp.concatenate([theirs, mine], 1))


def wide_body(tokens, gains, right_factors, left_factors):
    blocks_here, block_size = right_factors.shape[2:4]
    token_count, width_here = tokens.shape
    width = width_here * lax.axis_size("block")
    rounds = right_factors.shape[1]
    core = lax.axis_index("segment")
    count = lax.axis_size("segment")

    def gathered(value):
        return lax.all_gather(value[0], "segment", axis=0)

    gains, right_factors, left_factors = gathered(gains), gathered(right_factors), gathered(left_factors)
    current = tokens.T
    for layer in range(count * rounds):
        s, r = layer % count, layer // count
        sum_squares = lax.psum(jnp.sum(current * current, axis=0), "block")
        normed = current * lax.rsqrt(sum_squares / width + epsilon)[None, :] * gains[s, r][:, None]
        inner = jnp.einsum(
            "bit,bij->bjt",
            normed.reshape(blocks_here, block_size, token_count),
            right_factors[s, r],
            precision=exact,
        )
        combined = jnp.einsum(
            "bjt,jbc->cjt",
            lax.all_to_all(inner, "block", split_axis=1, concat_axis=0, tiled=True),
            left_factors[s, r],
            precision=exact,
        )
        mixed = lax.all_to_all(combined, "block", split_axis=0, concat_axis=1, tiled=True)
        current = current + mixed.reshape(width_here, token_count) * jax.nn.silu(normed)
    return current.T


def solution(mesh):
    placed = (
        P(("groups", "segment"), "block"),
        P("segment", None, "block"),
        P("segment", None, "block", None, None),
        P("segment", None, "block", None, None),
    )
    planes = dict(mesh.shape) == {"groups": 2, "segment": 2, "block": 8}

    def body(tokens, gains, right_factors, left_factors):
        fits = planes and tokens.shape == (256, 2048) and right_factors.shape[2:] == (16, 128, 128)
        return (plane_body if fits else wide_body)(tokens, gains, right_factors, left_factors)

    return jax.shard_map(
        body,
        mesh=mesh,
        in_specs=placed,
        out_specs=P(("groups", "segment"), "block"),
        check_vma=False,
    )
```

```python
import functools

import jax
import jax.numpy as jnp
from jax import lax
from jax.experimental import pallas as pl
from jax.experimental.pallas import tpu as pltpu
from jax.sharding import PartitionSpec as P

epsilon = 1e-06
exact = lax.Precision.HIGHEST
LANES = 128
ROWS = 8
PLANES = 4
QUARTERS = 4
CHUNKS = 2


def gray(position):
    return position ^ (position >> 1)


def row_offset(step, mate, position, quarter):
    start = gray((position + step) % PLANES) * (QUARTERS * ROWS) + (quarter ^ mate) * ROWS
    return pl.ds(pl.multiple_of(start, ROWS), ROWS)


def halves(value):
    high = value.astype(jnp.bfloat16)
    return high, (value - high.astype(jnp.float32)).astype(jnp.bfloat16)


def product(weight, value):
    def dot(a, b):
        return lax.dot_general(a, b, (((0,), (0,)), ((), ())), preferred_element_type=jnp.float32)

    weight_high, weight_low = halves(weight)
    value_high, value_low = halves(value)
    return dot(weight_high, value_high) + (dot(weight_high, value_low) + dot(weight_low, value_high))


def pick(piece, index, group):
    kind, base, refs = piece
    if kind == "whole":
        return refs[0][base + index]
    if kind == "halves":
        inside = base + index % 4
        owner = index // 4
    else:
        inside = base + index
        owner = 0 if kind == "next" else 1
    return jnp.where(group == owner, refs[0][inside], refs[1][inside])


def sent_tile(step, index, other, by_piece):
    if by_piece:
        return step, (other * ROWS + index) * ROWS
    return other // 2, ((other % 2) * 32 + step * ROWS + index) * ROWS


class Taker:
    def __init__(self, refs):
        self.refs = list(refs)

    def __call__(self, count):
        head, self.refs = self.refs[:count], self.refs[count:]
        return head


def read_place(place):
    return place[0], place[1], place[2]


def take_weights(take, kinds):
    return [(kind, base, take(1 if kind == "whole" else 2)) for kind, base in kinds]


def first_factor(steps, by_piece, current, gain, weights, send, tile, place):
    position, quarter, group = place
    squares = jnp.zeros((ROWS, LANES), jnp.float32)
    for n, step in enumerate(steps):
        for index in range(ROWS):
            value = current[n][index]
            squares += jnp.sum((value * value).reshape(LANES // ROWS, ROWS, LANES), axis=0)
            tile[index] = product(pick(weights[n], index, group), value * gain[n][index])
        for index in range(ROWS):
            for other in range(PLANES):
                for mate in range(QUARTERS):
                    part, start = sent_tile(step, index, other, by_piece)
                    ref = send[0 if by_piece else part][mate]
                    ref[pl.ds(start, ROWS), :] = tile[index, row_offset(other, mate, position, quarter), :]
    for ref in send[0]:
        ref[pl.ds(ref.shape[0] - ROWS, ROWS), :] = squares


def first_kernel(step, kinds, place, *refs):
    take = Taker(refs)
    tokens = take(1)[0]
    weights = take_weights(take, kinds)
    current, gain, rows, send, tile = take(1), take(1), take(1)[0], [take(QUARTERS)], take(1)[0]
    for index in range(ROWS):
        current[0][index] = tokens[pl.ds(0, LANES), pl.ds(index * LANES, LANES)].T
    rows[...] = tokens[pl.ds(LANES, ROWS), :]
    spread_gain(0, rows, gain[0])
    first_factor([step], True, current, gain, weights, send, tile, read_place(place))


def spread_gain(layer, rows, spread):
    for index in range(ROWS):
        columns = rows[:, pl.ds(index * LANES, LANES)].T
        spread[index] = jnp.broadcast_to(columns[:, layer : layer + 1], (LANES, LANES))


def deal_kernel(rounds, place, tokens, gains, their_tokens, their_gains, *pieces):
    position, core = place[0], place[1] % 2
    half = their_tokens.shape[1]
    columns = pl.ds(pl.multiple_of(core * half, half), half)
    rows = []
    for r in range(rounds):
        mine, other = gains[pl.ds(r, 1), columns], their_gains[pl.ds(r, 1), :]
        rows += [jnp.where(core == 0, mine, other), jnp.where(core == 0, other, mine)]
    rows.append(jnp.zeros((ROWS - 2 * rounds, half), jnp.float32))
    rows = jnp.concatenate(rows)
    for step in range(PLANES):
        plane = gray((position + PLANES - step) % PLANES)
        base = (plane % 2) * LANES

        def move(n, carry, step=step, plane=plane, base=base):
            start = pl.multiple_of(base + n * ROWS, ROWS)
            kept, other = tokens[pl.ds(start, ROWS), columns], their_tokens[pl.ds(start, ROWS), :]
            there = pl.ds(pl.multiple_of(n * ROWS, ROWS), ROWS)
            pieces[step][there, :] = jnp.where(plane // 2 == core, kept, other)
            return carry

        lax.fori_loop(0, LANES // ROWS, move, 0, unroll=4)
        pieces[step][pl.ds(LANES, ROWS), :] = rows


def last_kernel(width, step, squares_count, place, *refs):
    take = Taker(refs)
    position, quarter, _ = read_place(place)
    current, old_gain, squares_in, mixed = take(1)[0], take(1)[0], take(squares_count), take(QUARTERS)
    result, tile = take(2)
    scale = token_scale(width, squares_in)
    for index in range(ROWS):
        for other in range(PLANES):
            for mate in range(QUARTERS):
                where = row_offset(other, mate, position, quarter)
                _, start = sent_tile(step, index, other, True)
                mix = mixed[mate][pl.ds(start, ROWS), :]
                tile[index, where, :] = residual(current[index, where, :], mix, scale, old_gain[index, where, :])
        result[:, pl.ds(index * LANES, LANES)] = tile[index].T


def token_scale(width, squares):
    total = sum(ref[pl.ds(ref.shape[0] - ROWS, ROWS), :] for ref in squares)
    scale = lax.rsqrt(jnp.sum(total, axis=0, keepdims=True) / width + epsilon)
    return jnp.broadcast_to(scale, (ROWS, LANES))


def residual(value, mix, scale, gain):
    normed = value * scale * gain
    return value + (mix * scale) * (normed / (1.0 + jnp.exp(-normed)))


def edge_kernel(width, squares_count, kinds, place, *refs):
    take = Taker(refs)
    position, quarter, group = read_place(place)
    current, old_gain = take(PLANES), take(PLANES)
    squares_in = take(squares_count)
    mixed = [take(QUARTERS) for _ in range(CHUNKS)]
    gain = take(PLANES)
    weights = take_weights(take, kinds)
    fresh = take(PLANES)
    send, tile = [take(QUARTERS) for _ in range(CHUNKS)], take(1)[0]
    scale = token_scale(width, squares_in)
    for step in range(PLANES):

        def finish(index, carry, step=step):
            for other in range(PLANES):
                for mate in range(QUARTERS):
                    where = row_offset(other, mate, position, quarter)
                    value = current[step][index, where, :]
                    part, start = sent_tile(step, index, other, False)
                    mix = mixed[part][mate][pl.ds(pl.multiple_of(start, ROWS), ROWS), :]
                    gained = old_gain[step][index, where, :]
                    fresh[step][index, where, :] = residual(value, mix, scale, gained)
            return carry

        lax.fori_loop(0, ROWS, finish, 0, unroll=2)

    first_factor(range(PLANES), False, fresh, gain, weights, send, tile, (position, quarter, group))


def column_kernel(others, in_pieces, out_pieces, kinds, gain_layer, place, *refs):
    take = Taker(refs)
    position, quarter, group = read_place(place)
    came = [take(QUARTERS) for _ in range(PLANES if in_pieces else len(others) // 2)]
    weights = take_weights(take, kinds)
    rows = take(PLANES) if gain_layer else []
    send = [take(QUARTERS) for _ in range(PLANES if out_pieces else len(others) // 2)]
    spread = take(PLANES) if gain_layer else []
    value, tile = take(2)
    for n, other in enumerate(others):
        for index in range(ROWS):
            for step in range(PLANES):
                for mate in range(QUARTERS):
                    part, start = sent_tile(step, 0, other, in_pieces)
                    ref = came[part if in_pieces else n // 2][mate]
                    value[index, row_offset(step, mate, position, quarter), :] = ref[
                        pl.ds(start + index, ROWS, stride=ROWS), :
                    ]
            tile[index] = product(pick(weights[n], index, group), value[index])
            for step in range(PLANES):
                for mate in range(QUARTERS):
                    part, start = sent_tile(step, 0, other, out_pieces)
                    send[part if out_pieces else n // 2][mate][pl.ds(start + index, ROWS, stride=ROWS), :] = tile[
                        index, row_offset(step, mate, position, quarter), :
                    ]
    for step in range(len(rows)):
        spread_gain(gain_layer, rows[step], spread[step])


SMALL = pl.BlockSpec(memory_space=pltpu.SMEM)
WHOLE = pl.BlockSpec(memory_space=pltpu.VMEM)
PARAMS = pltpu.CompilerParams(vmem_limit_bytes=8 * 1024 * 1024)
PIECE = (ROWS, LANES, LANES)
COST_PART = 16


def array(*shape):
    return jax.ShapeDtypeStruct(shape, jnp.float32)


def marked(kernel, operand_count, wait_count, *refs):
    outs = refs[operand_count + wait_count :]
    outs[0][0] = 0
    kernel(*refs[:operand_count], *outs[1:])


def call(kernel, operands, outs, scratch, flops, waits=(), specs=None, out_spec=WHOLE):
    moved = 4 * (sum(a.size for a in operands) + sum(o.size for o in outs))
    results = pl.pallas_call(
        functools.partial(marked, kernel, len(operands), len(waits)),
        out_shape=[jax.ShapeDtypeStruct((1,), jnp.int32), *outs],
        in_specs=[SMALL] + (specs or [WHOLE] * (len(operands) - 1)) + [WHOLE if w.ndim > 1 else SMALL for w in waits],
        out_specs=[SMALL] + [out_spec] * len(outs),
        scratch_shapes=scratch if isinstance(scratch, list) else [pltpu.VMEM(PIECE, jnp.float32)] * scratch,
        compiler_params=PARAMS,
        cost_estimate=pl.CostEstimate(flops=flops // COST_PART, bytes_accessed=moved // COST_PART, transcendentals=0),
    )(*operands, *waits)
    return list(results[1:]), results[0]


def copies_kernel(moves, in_count, out_count, place, *refs):
    sems = refs[-1]
    copies = []
    for n, (source, at, target, there, when) in enumerate(moves):
        copy = pltpu.make_async_copy(refs[source].at[at(place)], refs[in_count + target].at[there], sems.at[n])
        copies.append((copy, when))
    for act in ("start", "wait"):
        for copy, when in copies:
            if when is None:
                getattr(copy, act)()
            else:
                pl.when(when(place))(getattr(copy, act))


def copied(place, operands, outs, moves, waits=(), anywhere=True):
    specs = [pl.BlockSpec(memory_space=pl.ANY) if anywhere else WHOLE] * len(operands)
    kernel = functools.partial(copies_kernel, moves, len(operands), len(outs))
    sems = [pltpu.SemaphoreType.DMA((len(moves),))]
    return call(kernel, [place, *operands], outs, sems, 0, waits, specs)[0]


def core_of(place):
    return place[1] % 2


STAGE_FLOPS = 6 * 32 * LANES * LANES * LANES


def split_weights(weights):
    return [array for piece in weights for array in piece[2]], [piece[:2] for piece in weights]


def deal(place, tokens, gains, their_tokens, their_gains):
    outs = [array(LANES + ROWS, their_tokens.shape[1])] * PLANES
    operands = [place, tokens, gains, their_tokens, their_gains]
    return call(functools.partial(deal_kernel, gains.shape[0]), operands, outs, 0, 0)


def first_piece(step, place, tokens, weights, waits):
    operands, kinds = split_weights([weights])
    kernel = functools.partial(first_kernel, step, kinds)
    outs = [array(*PIECE)] * 2 + [array(ROWS, ROWS * LANES)] + [array(264, LANES)] * QUARTERS
    results, mark = call(kernel, [place, tokens, *operands], outs, 1, STAGE_FLOPS // 4, waits)
    return results[:3], results[3:], mark


def last_piece(width, step, place, current, old_gain, squares, mixed):
    kernel = functools.partial(last_kernel, width, step, len(squares))
    operands = [place, current, old_gain, *squares, *mixed]
    return call(kernel, operands, [array(LANES, ROWS * LANES)], 1, STAGE_FLOPS // 4)[0][0]


def layer_edge(width, place, current, old_gain, squares, mixed, gain, weights):
    more, kinds = split_weights(weights)
    operands = [place, *current, *old_gain, *squares, *mixed[0], *mixed[1], *gain, *more]
    outs = [array(*PIECE)] * PLANES + [array(520, LANES)] * QUARTERS + [array(512, LANES)] * QUARTERS
    kernel = functools.partial(edge_kernel, width, len(squares), kinds)
    results, _ = call(kernel, operands, outs, 1, 2 * STAGE_FLOPS)
    return results[:PLANES], [results[PLANES : PLANES + QUARTERS], results[PLANES + QUARTERS :]]


def column_stage(others, in_pieces, out_pieces, place, came, weights, rows=(), gain_layer=0):
    more, kinds = split_weights(weights)
    operands = [place, *(ref for part in came for ref in part), *more, *rows]
    outs = [array(256, LANES)] * (QUARTERS * PLANES) if out_pieces else [array(512, LANES)] * QUARTERS
    count = len(outs)
    outs = outs + [array(*PIECE)] * len(rows)
    kernel = functools.partial(column_kernel, others, in_pieces, out_pieces, kinds, gain_layer)
    results, mark = call(kernel, operands, outs, 2, STAGE_FLOPS)
    return [results[n : n + QUARTERS] for n in range(0, count, QUARTERS)], results[count:], mark


def routed(value, to):
    route = []
    for core in range(2):
        for z in range(PLANES):
            for y in range(2):
                there = to(core, z, y)
                route.append((core * 8 + z * 2 + y, there[0] * 8 + there[1] * 2 + there[2]))
    return lax.ppermute(value, ("segment", "block"), route)


def core_swap(value):
    return routed(value, lambda core, z, y: (1 - core, z, y))


def ring(value, distance):
    return routed(value, lambda core, z, y: (core, gray((gray(z) + distance) % PLANES), y))


def group_ring(value):
    route = []
    for group in range(2):
        for core in range(2):
            for z in range(PLANES):
                for y in range(2):
                    there = gray((gray(z) + (1 if group else -1)) % PLANES)
                    start = group * 16 + core * 8 + y
                    route.append((start + z * 2, start + there * 2))
    return lax.ppermute(value, ("groups", "segment", "block"), route)


def to_mate(value, mate):
    return routed(value, lambda core, z, y: (core ^ (mate & 1), z, y ^ (mate >> 1)))


def group_swap(value):
    return lax.ppermute(value, "groups", [(0, 1), (1, 0)])


def exchange(chunk):
    return [chunk[0]] + [to_mate(chunk[mate], mate) for mate in range(1, QUARTERS)]


def plane_body(tokens, gains, right_factors, left_factors):
    core = lax.axis_index("segment")
    block = lax.axis_index("block")
    group = lax.axis_index("groups")
    z, y = block // 2, block % 2
    position = gray(z)
    place = jnp.stack([position, y * 2 + core, group]).astype(jnp.int32)
    rounds = right_factors.shape[1]
    layers = 2 * rounds
    width = right_factors.shape[3] * 8 * right_factors.shape[2]

    count, half = tokens.shape[0], tokens.shape[1] // 2
    their_tokens = core_swap(lax.dynamic_slice_in_dim(tokens, (1 - core) * half, half, 1))
    their_gains = core_swap(lax.dynamic_slice_in_dim(gains[0], (1 - core) * half, half, 1))

    pieces, dealt = deal(place, tokens, gains[0], their_tokens, their_gains)
    arrived = [piece if step == 0 else ring(piece, -step) for step, piece in enumerate(pieces)]

    def swapped(factors, r, waits):
        move = (0, lambda p: (0, r, pl.ds((1 - core_of(p)) * ROWS, ROWS)), 0, pl.ds(0, ROWS), None)
        return factors, r, core_swap(copied(place, [factors], [array(*PIECE)], [move], waits)[0])

    def own(pairs, section, waits):
        operands, moves = [], []
        for n, (factors, r, theirs) in enumerate(pairs):
            there = pl.ds(n * ROWS, ROWS)
            operands += [factors, theirs]
            mine = lambda p, r=r: (0, r, pl.ds(core_of(p) * ROWS, ROWS))
            moves.append((2 * n, mine, 0, there, lambda p: core_of(p) == section))
            moves.append((2 * n + 1, lambda p: pl.ds(0, ROWS), 0, there, lambda p: core_of(p) != section))
        return copied(place, operands, [array(len(pairs) * ROWS, LANES, LANES)], moves, waits)[0]

    def near_half(near, waits=()):
        count = near.shape[0] // ROWS
        moves = [
            (0, lambda p, n=n: pl.ds(n * ROWS + p[2] * 4, 4), 0, pl.ds(n * 4, 4), None) for n in range(count)
        ]
        return group_ring(copied(place, [near], [array(count * 4, LANES, LANES)], moves, waits, False)[0])

    def four_pieces(part, near, far):
        near_pair, far_pair = (near, group_swap(near)), (far, group_swap(far))
        return [
            [
                ("whole", n * ROWS, (part,)),
                ("next", n * ROWS, near_pair),
                ("halves", n * 4, far_pair),
                ("previous", n * ROWS, near_pair),
            ]
            for n in range(part.shape[0] // ROWS)
        ]

    right_parts, left_parts = [None] * layers, [None] * layers
    pairs = [swapped(right_factors, 0, ())]
    part = own(pairs, 0, ())
    near = group_ring(part)
    far = near_half(near, arrived[1:4:2])
    (right_parts[0],) = four_pieces(part, near, far)
    pairs.append(swapped(left_factors, 0, [dealt]))

    current, gain, rows, came = [None] * PLANES, [None] * PLANES, [None] * PLANES, [None] * PLANES
    waits = []
    for step in (0, 1, 3, 2):
        results, sends, mark = first_piece(step, place, arrived[step], right_parts[0][step], waits)
        waits = [mark]
        current[step], gain[step], rows[step] = results
        came[step] = exchange(sends)
    part = own(pairs[1:], 0, [arrived[2], far])
    near = group_ring(part)
    far = near_half(near)
    (left_parts[0],) = four_pieces(part, near, far)
    for layer in range(layers - 1):
        part = own(pairs, (layer + 1) % 2, [far, mark])
        near = group_ring(part)
        far = near_half(near)
        right_parts[layer + 1], left_parts[layer + 1] = four_pieces(part, near, far)
        in_pieces = layer == 0
        squares = [part[mate] for part in (came if in_pieces else came[:1]) for mate in range(QUARTERS)]
        mixed = []
        for chunk in range(CHUNKS):
            others = (chunk * 2, chunk * 2 + 1)
            extra = (rows, layer + 1) if chunk == 0 else ()
            weights = left_parts[layer][others[0] : others[1] + 1]
            source = came if in_pieces else came[chunk : chunk + 1]
            (half_sends,), spread, mark = column_stage(others, in_pieces, False, place, source, weights, *extra)
            mixed.append(exchange(half_sends))
            next_gain = spread or next_gain
        if layer % 2 == 0 and layer + 2 < layers:
            pairs = [swapped(factors, (layer + 2) // 2, [mark]) for factors in (right_factors, left_factors)]
        current, sends = layer_edge(
            width, place, current, gain, squares, mixed, next_gain, right_parts[layer + 1]
        )
        gain = next_gain
        came = [exchange(sends[0]), exchange(sends[1])]

    squares = came[0]
    sends, _, _ = column_stage(tuple(range(PLANES)), False, True, place, came, left_parts[-1])
    back = [None] * PLANES
    for step in (2, 1, 3, 0):
        mixed = exchange(sends[step])
        done = last_piece(width, step, place, current[step], gain[step], squares, mixed)
        back[step] = done if step == 0 else ring(done, step)
    stacked = jnp.stack(back)

    def found_for(half_index):
        planes = [half_index * 2 + n for n in range(2)]
        return jnp.stack(
            [lax.dynamic_index_in_dim(stacked, (position - gray(p)) % PLANES, 0, keepdims=False) for p in planes]
        ).reshape(tokens.shape[0], half)

    mine = found_for(core)
    theirs = core_swap(found_for(1 - core))
    return jnp.where(core == 0, jnp.concatenate([mine, theirs], 1), jnp.concatenate([theirs, mine], 1))


def wide_body(tokens, gains, right_factors, left_factors):
    blocks_here, block_size = right_factors.shape[2:4]
    token_count, width_here = tokens.shape
    width = width_here * lax.axis_size("block")
    rounds = right_factors.shape[1]
    core = lax.axis_index("segment")
    count = lax.axis_size("segment")

    def gathered(value):
        return lax.all_gather(value[0], "segment", axis=0)

    gains, right_factors, left_factors = gathered(gains), gathered(right_factors), gathered(left_factors)
    current = tokens.T
    for layer in range(count * rounds):
        s, r = layer % count, layer // count
        sum_squares = lax.psum(jnp.sum(current * current, axis=0), "block")
        normed = current * lax.rsqrt(sum_squares / width + epsilon)[None, :] * gains[s, r][:, None]
        inner = jnp.einsum(
            "bit,bij->bjt",
            normed.reshape(blocks_here, block_size, token_count),
            right_factors[s, r],
            precision=exact,
        )
        combined = jnp.einsum(
            "bjt,jbc->cjt",
            lax.all_to_all(inner, "block", split_axis=1, concat_axis=0, tiled=True),
            left_factors[s, r],
            precision=exact,
        )
        mixed = lax.all_to_all(combined, "block", split_axis=0, concat_axis=1, tiled=True)
        current = current + mixed.reshape(width_here, token_count) * jax.nn.silu(normed)
    return current.T


def solution(mesh):
    placed = (
        P(("groups", "segment"), "block"),
        P("segment", None, "block"),
        P("segment", None, "block", None, None),
        P("segment", None, "block", None, None),
    )
    planes = dict(mesh.shape) == {"groups": 2, "segment": 2, "block": 8}

    def body(tokens, gains, right_factors, left_factors):
        fits = planes and tokens.shape == (256, 2048) and right_factors.shape[2:] == (16, 128, 128)
        return (plane_body if fits else wide_body)(tokens, gains, right_factors, left_factors)

    return jax.shard_map(
        body,
        mesh=mesh,
        in_specs=placed,
        out_specs=P(("groups", "segment"), "block"),
        check_vma=False,
    )
```

```python
import functools

import jax
import jax.numpy as jnp
from jax import lax
from jax.experimental import pallas as pl
from jax.experimental.pallas import tpu as pltpu
from jax.sharding import PartitionSpec as P

epsilon = 1e-06
exact = lax.Precision.HIGHEST
LANES = 128
ROWS = 8
PLANES = 4
QUARTERS = 4
CHUNKS = 2


def gray(position):
    return position ^ (position >> 1)


def row_offset(step, mate, position, quarter):
    start = gray((position + step) % PLANES) * (QUARTERS * ROWS) + (quarter ^ mate) * ROWS
    return pl.ds(pl.multiple_of(start, ROWS), ROWS)


def halves(value):
    high = value.astype(jnp.bfloat16)
    return high, (value - high.astype(jnp.float32)).astype(jnp.bfloat16)


def product(weight, value):
    def dot(a, b):
        return lax.dot_general(a, b, (((0,), (0,)), ((), ())), preferred_element_type=jnp.float32)

    weight_high, weight_low = halves(weight)
    value_high, value_low = halves(value)
    return dot(weight_high, value_high) + (dot(weight_high, value_low) + dot(weight_low, value_high))


def pick(piece, index, group):
    kind, base, refs = piece
    if kind == "whole":
        return refs[0][base + index]
    if kind == "halves":
        inside = base + index % 4
        owner = index // 4
    else:
        inside = base + index
        owner = 0 if kind == "next" else 1
    return jnp.where(group == owner, refs[0][inside], refs[1][inside])


def sent_tile(step, index, other, by_piece):
    if by_piece:
        return step, (other * ROWS + index) * ROWS
    return other // 2, ((other % 2) * 32 + step * ROWS + index) * ROWS


class Taker:
    def __init__(self, refs):
        self.refs = list(refs)

    def __call__(self, count):
        head, self.refs = self.refs[:count], self.refs[count:]
        return head


def read_place(place):
    return place[0], place[1], place[2]


def take_weights(take, kinds):
    return [(kind, base, take(1 if kind == "whole" else 2)) for kind, base in kinds]


def first_factor(steps, by_piece, current, gain, weights, send, tile, place):
    position, quarter, group = place
    squares = jnp.zeros((ROWS, LANES), jnp.float32)
    for n, step in enumerate(steps):
        for index in range(ROWS):
            value = current[n][index]
            squares += jnp.sum((value * value).reshape(LANES // ROWS, ROWS, LANES), axis=0)
            tile[index] = product(pick(weights[n], index, group), value * gain[n][index])
        for index in range(ROWS):
            for other in range(PLANES):
                for mate in range(QUARTERS):
                    part, start = sent_tile(step, index, other, by_piece)
                    ref = send[0 if by_piece else part][mate]
                    ref[pl.ds(start, ROWS), :] = tile[index, row_offset(other, mate, position, quarter), :]
    for ref in send[0]:
        ref[pl.ds(ref.shape[0] - ROWS, ROWS), :] = squares


def first_kernel(step, kinds, place, *refs):
    take = Taker(refs)
    tokens = take(1)[0]
    weights = take_weights(take, kinds)
    current, gain, rows, send, tile = take(1), take(1), take(1)[0], [take(QUARTERS)], take(1)[0]
    for index in range(ROWS):
        current[0][index] = tokens[pl.ds(0, LANES), pl.ds(index * LANES, LANES)].T
    rows[...] = tokens[pl.ds(LANES, ROWS), :]
    spread_gain(0, rows, gain[0])
    first_factor([step], True, current, gain, weights, send, tile, read_place(place))


def spread_gain(layer, rows, spread):
    for index in range(ROWS):
        columns = rows[:, pl.ds(index * LANES, LANES)].T
        spread[index] = jnp.broadcast_to(columns[:, layer : layer + 1], (LANES, LANES))


def deal_kernel(rounds, place, tokens, gains, their_tokens, their_gains, *pieces):
    position, core = place[0], place[1] % 2
    half = their_tokens.shape[1]
    columns = pl.ds(pl.multiple_of(core * half, half), half)
    rows = []
    for r in range(rounds):
        mine, other = gains[pl.ds(r, 1), columns], their_gains[pl.ds(r, 1), :]
        rows += [jnp.where(core == 0, mine, other), jnp.where(core == 0, other, mine)]
    rows.append(jnp.zeros((ROWS - 2 * rounds, half), jnp.float32))
    rows = jnp.concatenate(rows)
    for step in range(PLANES):
        plane = gray((position + PLANES - step) % PLANES)
        base = (plane % 2) * LANES

        def move(n, carry, step=step, plane=plane, base=base):
            start = pl.multiple_of(base + n * ROWS, ROWS)
            kept, other = tokens[pl.ds(start, ROWS), columns], their_tokens[pl.ds(start, ROWS), :]
            there = pl.ds(pl.multiple_of(n * ROWS, ROWS), ROWS)
            pieces[step][there, :] = jnp.where(plane // 2 == core, kept, other)
            return carry

        lax.fori_loop(0, LANES // ROWS, move, 0, unroll=4)
        pieces[step][pl.ds(LANES, ROWS), :] = rows


def last_kernel(width, step, squares_count, place, *refs):
    take = Taker(refs)
    position, quarter, _ = read_place(place)
    current, old_gain, squares_in, mixed = take(1)[0], take(1)[0], take(squares_count), take(QUARTERS)
    result, tile = take(2)
    scale = token_scale(width, squares_in)
    for index in range(ROWS):
        for other in range(PLANES):
            for mate in range(QUARTERS):
                where = row_offset(other, mate, position, quarter)
                _, start = sent_tile(step, index, other, True)
                mix = mixed[mate][pl.ds(start, ROWS), :]
                tile[index, where, :] = residual(current[index, where, :], mix, scale, old_gain[index, where, :])
        result[:, pl.ds(index * LANES, LANES)] = tile[index].T


def token_scale(width, squares):
    total = sum(ref[pl.ds(ref.shape[0] - ROWS, ROWS), :] for ref in squares)
    scale = lax.rsqrt(jnp.sum(total, axis=0, keepdims=True) / width + epsilon)
    return jnp.broadcast_to(scale, (ROWS, LANES))


def residual(value, mix, scale, gain):
    normed = value * scale * gain
    return value + (mix * scale) * (normed / (1.0 + jnp.exp(-normed)))


def edge_kernel(width, squares_count, kinds, place, *refs):
    take = Taker(refs)
    position, quarter, group = read_place(place)
    current, old_gain = take(PLANES), take(PLANES)
    squares_in = take(squares_count)
    mixed = [take(QUARTERS) for _ in range(CHUNKS)]
    gain = take(PLANES)
    weights = take_weights(take, kinds)
    fresh = take(PLANES)
    send, tile = [take(QUARTERS) for _ in range(CHUNKS)], take(1)[0]
    scale = token_scale(width, squares_in)
    for step in range(PLANES):

        def finish(index, carry, step=step):
            for other in range(PLANES):
                for mate in range(QUARTERS):
                    where = row_offset(other, mate, position, quarter)
                    value = current[step][index, where, :]
                    part, start = sent_tile(step, index, other, False)
                    mix = mixed[part][mate][pl.ds(pl.multiple_of(start, ROWS), ROWS), :]
                    gained = old_gain[step][index, where, :]
                    fresh[step][index, where, :] = residual(value, mix, scale, gained)
            return carry

        lax.fori_loop(0, ROWS, finish, 0, unroll=2)

    first_factor(range(PLANES), False, fresh, gain, weights, send, tile, (position, quarter, group))


def column_kernel(others, in_pieces, out_pieces, kinds, gain_layer, place, *refs):
    take = Taker(refs)
    position, quarter, group = read_place(place)
    came = [take(QUARTERS) for _ in range(PLANES if in_pieces else len(others) // 2)]
    weights = take_weights(take, kinds)
    rows = take(PLANES) if gain_layer else []
    send = [take(QUARTERS) for _ in range(PLANES if out_pieces else len(others) // 2)]
    spread = take(PLANES) if gain_layer else []
    value, tile = take(2)
    for n, other in enumerate(others):
        for index in range(ROWS):
            for step in range(PLANES):
                for mate in range(QUARTERS):
                    part, start = sent_tile(step, 0, other, in_pieces)
                    ref = came[part if in_pieces else n // 2][mate]
                    value[index, row_offset(step, mate, position, quarter), :] = ref[
                        pl.ds(start + index, ROWS, stride=ROWS), :
                    ]
            tile[index] = product(pick(weights[n], index, group), value[index])
            for step in range(PLANES):
                for mate in range(QUARTERS):
                    part, start = sent_tile(step, 0, other, out_pieces)
                    send[part if out_pieces else n // 2][mate][pl.ds(start + index, ROWS, stride=ROWS), :] = tile[
                        index, row_offset(step, mate, position, quarter), :
                    ]
    for step in range(len(rows)):
        spread_gain(gain_layer, rows[step], spread[step])


SMALL = pl.BlockSpec(memory_space=pltpu.SMEM)
WHOLE = pl.BlockSpec(memory_space=pltpu.VMEM)
PARAMS = pltpu.CompilerParams(vmem_limit_bytes=8 * 1024 * 1024)
PIECE = (ROWS, LANES, LANES)
COST_PART = 16


def array(*shape):
    return jax.ShapeDtypeStruct(shape, jnp.float32)


def marked(kernel, operand_count, wait_count, *refs):
    outs = refs[operand_count + wait_count :]
    outs[0][0] = 0
    kernel(*refs[:operand_count], *outs[1:])


def call(kernel, operands, outs, scratch, flops, waits=(), specs=None, out_spec=WHOLE):
    moved = 4 * (sum(a.size for a in operands) + sum(o.size for o in outs))
    results = pl.pallas_call(
        functools.partial(marked, kernel, len(operands), len(waits)),
        out_shape=[jax.ShapeDtypeStruct((1,), jnp.int32), *outs],
        in_specs=[SMALL] + (specs or [WHOLE] * (len(operands) - 1)) + [WHOLE if w.ndim > 1 else SMALL for w in waits],
        out_specs=[SMALL] + [out_spec] * len(outs),
        scratch_shapes=scratch if isinstance(scratch, list) else [pltpu.VMEM(PIECE, jnp.float32)] * scratch,
        compiler_params=PARAMS,
        cost_estimate=pl.CostEstimate(flops=flops // COST_PART, bytes_accessed=moved // COST_PART, transcendentals=0),
    )(*operands, *waits)
    return list(results[1:]), results[0]


def copies_kernel(moves, in_count, out_count, place, *refs):
    sems = refs[-1]
    copies = []
    for n, (source, at, target, there, when) in enumerate(moves):
        copy = pltpu.make_async_copy(refs[source].at[at(place)], refs[in_count + target].at[there], sems.at[n])
        copies.append((copy, when))
    for act in ("start", "wait"):
        for copy, when in copies:
            if when is None:
                getattr(copy, act)()
            else:
                pl.when(when(place))(getattr(copy, act))


def copied(place, operands, outs, moves, waits=(), anywhere=True):
    specs = [pl.BlockSpec(memory_space=pl.ANY) if anywhere else WHOLE] * len(operands)
    kernel = functools.partial(copies_kernel, moves, len(operands), len(outs))
    sems = [pltpu.SemaphoreType.DMA((len(moves),))]
    return call(kernel, [place, *operands], outs, sems, 0, waits, specs)[0]


def core_of(place):
    return place[1] % 2


STAGE_FLOPS = 6 * 32 * LANES * LANES * LANES


def split_weights(weights):
    return [array for piece in weights for array in piece[2]], [piece[:2] for piece in weights]


def deal(place, tokens, gains, their_tokens, their_gains):
    outs = [array(LANES + ROWS, their_tokens.shape[1])] * PLANES
    operands = [place, tokens, gains, their_tokens, their_gains]
    return call(functools.partial(deal_kernel, gains.shape[0]), operands, outs, 0, 0)


def first_piece(step, place, tokens, weights, waits):
    operands, kinds = split_weights([weights])
    kernel = functools.partial(first_kernel, step, kinds)
    outs = [array(*PIECE)] * 2 + [array(ROWS, ROWS * LANES)] + [array(264, LANES)] * QUARTERS
    results, mark = call(kernel, [place, tokens, *operands], outs, 1, STAGE_FLOPS // 4, waits)
    return results[:3], results[3:], mark


def last_piece(width, step, place, current, old_gain, squares, mixed):
    kernel = functools.partial(last_kernel, width, step, len(squares))
    operands = [place, current, old_gain, *squares, *mixed]
    return call(kernel, operands, [array(LANES, ROWS * LANES)], 1, STAGE_FLOPS // 4)[0][0]


def layer_edge(width, place, current, old_gain, squares, mixed, gain, weights):
    more, kinds = split_weights(weights)
    operands = [place, *current, *old_gain, *squares, *mixed[0], *mixed[1], *gain, *more]
    outs = [array(*PIECE)] * PLANES + [array(520, LANES)] * QUARTERS + [array(512, LANES)] * QUARTERS
    kernel = functools.partial(edge_kernel, width, len(squares), kinds)
    results, mark = call(kernel, operands, outs, 1, 2 * STAGE_FLOPS)
    return results[:PLANES], [results[PLANES : PLANES + QUARTERS], results[PLANES + QUARTERS :]], mark


def column_stage(others, in_pieces, out_pieces, place, came, weights, waits, rows=(), gain_layer=0):
    more, kinds = split_weights(weights)
    operands = [place, *(ref for part in came for ref in part), *more, *rows]
    outs = [array(256, LANES)] * (QUARTERS * PLANES) if out_pieces else [array(512, LANES)] * QUARTERS
    count = len(outs)
    outs = outs + [array(*PIECE)] * len(rows)
    kernel = functools.partial(column_kernel, others, in_pieces, out_pieces, kinds, gain_layer)
    results, mark = call(kernel, operands, outs, 2, STAGE_FLOPS, waits)
    return [results[n : n + QUARTERS] for n in range(0, count, QUARTERS)], results[count:], mark


def routed(value, to):
    route = []
    for core in range(2):
        for z in range(PLANES):
            for y in range(2):
                there = to(core, z, y)
                route.append((core * 8 + z * 2 + y, there[0] * 8 + there[1] * 2 + there[2]))
    return lax.ppermute(value, ("segment", "block"), route)


def core_swap(value):
    return routed(value, lambda core, z, y: (1 - core, z, y))


def ring(value, distance):
    return routed(value, lambda core, z, y: (core, gray((gray(z) + distance) % PLANES), y))


def group_ring(value):
    route = []
    for group in range(2):
        for core in range(2):
            for z in range(PLANES):
                for y in range(2):
                    there = gray((gray(z) + (1 if group else -1)) % PLANES)
                    start = group * 16 + core * 8 + y
                    route.append((start + z * 2, start + there * 2))
    return lax.ppermute(value, ("groups", "segment", "block"), route)


def to_mate(value, mate):
    return routed(value, lambda core, z, y: (core ^ (mate & 1), z, y ^ (mate >> 1)))


def group_swap(value):
    return lax.ppermute(value, "groups", [(0, 1), (1, 0)])


def exchange(chunk):
    return [chunk[0]] + [to_mate(chunk[mate], mate) for mate in range(1, QUARTERS)]


def plane_body(tokens, gains, right_factors, left_factors):
    core = lax.axis_index("segment")
    block = lax.axis_index("block")
    group = lax.axis_index("groups")
    z, y = block // 2, block % 2
    position = gray(z)
    place = jnp.stack([position, y * 2 + core, group]).astype(jnp.int32)
    rounds = right_factors.shape[1]
    layers = 2 * rounds
    width = right_factors.shape[3] * 8 * right_factors.shape[2]

    count, half = tokens.shape[0], tokens.shape[1] // 2
    their_tokens = core_swap(lax.dynamic_slice_in_dim(tokens, (1 - core) * half, half, 1))
    their_gains = core_swap(lax.dynamic_slice_in_dim(gains[0], (1 - core) * half, half, 1))

    pieces, dealt = deal(place, tokens, gains[0], their_tokens, their_gains)
    arrived = [piece if step == 0 else ring(piece, -step) for step, piece in enumerate(pieces)]

    def swapped(factors, r, waits):
        move = (0, lambda p: (0, r, pl.ds((1 - core_of(p)) * ROWS, ROWS)), 0, pl.ds(0, ROWS), None)
        return factors, r, core_swap(copied(place, [factors], [array(*PIECE)], [move], waits)[0])

    def own(pairs, section, waits):
        operands, moves = [], []
        for n, (factors, r, theirs) in enumerate(pairs):
            there = pl.ds(n * ROWS, ROWS)
            operands += [factors, theirs]
            mine = lambda p, r=r: (0, r, pl.ds(core_of(p) * ROWS, ROWS))
            moves.append((2 * n, mine, 0, there, lambda p: core_of(p) == section))
            moves.append((2 * n + 1, lambda p: pl.ds(0, ROWS), 0, there, lambda p: core_of(p) != section))
        return copied(place, operands, [array(len(pairs) * ROWS, LANES, LANES)], moves, waits)[0]

    def near_half(near, waits=()):
        count = near.shape[0] // ROWS
        moves = [
            (0, lambda p, n=n: pl.ds(n * ROWS + p[2] * 4, 4), 0, pl.ds(n * 4, 4), None) for n in range(count)
        ]
        moves.append((0, lambda p: pl.ds(0, count * ROWS), 1, pl.ds(0, count * ROWS), None))
        outs = [array(count * 4, LANES, LANES), array(count * ROWS, LANES, LANES)]
        passed, kept = copied(place, [near], outs, moves, waits, False)
        return group_ring(passed), kept

    def four_pieces(part, far, near):
        near_pair, far_pair = (near, group_swap(near)), (far, group_swap(far))
        return [
            [
                ("whole", n * ROWS, (part,)),
                ("next", n * ROWS, near_pair),
                ("halves", n * 4, far_pair),
                ("previous", n * ROWS, near_pair),
            ]
            for n in range(part.shape[0] // ROWS)
        ]

    right_parts, left_parts = [None] * layers, [None] * layers
    pairs = [swapped(right_factors, 0, ())]
    part = own(pairs, 0, ())
    near = group_ring(part)
    pairs.append(swapped(left_factors, 0, [dealt]))

    current, gain, rows, came = [None] * PLANES, [None] * PLANES, [None] * PLANES, [None] * PLANES
    waits = []
    for step in (0, 1, 3, 2):
        if step == 1:
            far, near = near_half(near, [*arrived[1:4:2], mark])
            (right_parts[0],) = four_pieces(part, far, near)
        weights = right_parts[0][step] if step else ("whole", 0, (part,))
        results, sends, mark = first_piece(step, place, arrived[step], weights, waits)
        waits = [mark]
        current[step], gain[step], rows[step] = results
        came[step] = exchange(sends)
        if step == 3:
            left = own(pairs[1:], 0, [arrived[2], far, mark, *came[0][2:], *came[1][2:]])
            left_near = group_ring(left)
    far, near = near_half(left_near, [mark, *came[3][2:]])
    (left_parts[0],) = four_pieces(left, far, near)
    right = own(pairs[:1], 1, [far, *came[2][2:], left_parts[0][1][2][1]])
    right_near = group_ring(right)
    left = own(pairs[1:], 1, [right])
    left_near = group_ring(left)
    for layer in range(layers - 1):
        in_pieces = layer == 0
        squares = [part[mate] for part in (came if in_pieces else came[:1]) for mate in range(QUARTERS)]
        mixed, marks = [], []
        for chunk in range(CHUNKS):
            others = (chunk * 2, chunk * 2 + 1)
            extra = (rows, layer + 1) if chunk == 0 else ()
            weights = left_parts[layer][others[0] : others[1] + 1]
            source = came if in_pieces else came[chunk : chunk + 1]
            (half_sends,), spread, mark = column_stage(
                others, in_pieces, False, place, source, weights, marks, *extra
            )
            mixed.append(exchange(half_sends))
            marks = [mark]
            next_gain = spread or next_gain
        if layer == 0:
            far, near = near_half(right_near, marks)
            (right_parts[1],) = four_pieces(right, far, near)
            right_last = right_parts[1][2][2][1]
            far, near = near_half(left_near, [far, right_parts[1][1][2][1], *mixed[0][2:]])
            (left_parts[1],) = four_pieces(left, far, near)
            pairs = [swapped(factors, 1, marks) for factors in (right_factors, left_factors)]
        if layer + 2 < layers:
            waits = [far, mark if layer else right_last, *mixed[0][2:], *mixed[1][2:]]
            part = own(pairs, layer % 2, waits)
            near = group_ring(part)
        current, sends, mark = layer_edge(
            width, place, current, gain, squares, mixed, next_gain, right_parts[layer + 1]
        )
        gain = next_gain
        came = [exchange(sends[0]), exchange(sends[1])]
        if layer + 2 < layers:
            waits = ()
            if layer == 0:
                swaps = left_parts[1][1][2][1], left_parts[1][2][2][1]
                waits = [mark, *came[0][2:], *swaps]
            far, kept = near_half(near, waits)
            near = near if layer else kept
            right_parts[layer + 2], left_parts[layer + 2] = four_pieces(part, far, near)

    squares = came[0]
    sends, _, _ = column_stage(tuple(range(PLANES)), False, True, place, came, left_parts[-1], ())
    back = [None] * PLANES
    for step in (2, 1, 3, 0):
        mixed = exchange(sends[step])
        done = last_piece(width, step, place, current[step], gain[step], squares, mixed)
        back[step] = done if step == 0 else ring(done, step)
    stacked = jnp.stack(back)

    def found_for(half_index):
        planes = [half_index * 2 + n for n in range(2)]
        return jnp.stack(
            [lax.dynamic_index_in_dim(stacked, (position - gray(p)) % PLANES, 0, keepdims=False) for p in planes]
        ).reshape(tokens.shape[0], half)

    mine = found_for(core)
    theirs = core_swap(found_for(1 - core))
    return jnp.where(core == 0, jnp.concatenate([mine, theirs], 1), jnp.concatenate([theirs, mine], 1))


def wide_body(tokens, gains, right_factors, left_factors):
    blocks_here, block_size = right_factors.shape[2:4]
    token_count, width_here = tokens.shape
    width = width_here * lax.axis_size("block")
    rounds = right_factors.shape[1]
    core = lax.axis_index("segment")
    count = lax.axis_size("segment")

    def gathered(value):
        return lax.all_gather(value[0], "segment", axis=0)

    gains, right_factors, left_factors = gathered(gains), gathered(right_factors), gathered(left_factors)
    current = tokens.T
    for layer in range(count * rounds):
        s, r = layer % count, layer // count
        sum_squares = lax.psum(jnp.sum(current * current, axis=0), "block")
        normed = current * lax.rsqrt(sum_squares / width + epsilon)[None, :] * gains[s, r][:, None]
        inner = jnp.einsum(
            "bit,bij->bjt",
            normed.reshape(blocks_here, block_size, token_count),
            right_factors[s, r],
            precision=exact,
        )
        combined = jnp.einsum(
            "bjt,jbc->cjt",
            lax.all_to_all(inner, "block", split_axis=1, concat_axis=0, tiled=True),
            left_factors[s, r],
            precision=exact,
        )
        mixed = lax.all_to_all(combined, "block", split_axis=0, concat_axis=1, tiled=True)
        current = current + mixed.reshape(width_here, token_count) * jax.nn.silu(normed)
    return current.T


def solution(mesh):
    placed = (
        P(("groups", "segment"), "block"),
        P("segment", None, "block"),
        P("segment", None, "block", None, None),
        P("segment", None, "block", None, None),
    )
    planes = dict(mesh.shape) == {"groups": 2, "segment": 2, "block": 8}

    def body(tokens, gains, right_factors, left_factors):
        fits = planes and tokens.shape == (256, 2048) and right_factors.shape[2:] == (16, 128, 128)
        return (plane_body if fits else wide_body)(tokens, gains, right_factors, left_factors)

    return jax.shard_map(
        body,
        mesh=mesh,
        in_specs=placed,
        out_specs=P(("groups", "segment"), "block"),
        check_vma=False,
    )
```

```python
import functools

import jax
import jax.numpy as jnp
from jax import lax
from jax.experimental import pallas as pl
from jax.experimental.pallas import tpu as pltpu
from jax.sharding import PartitionSpec as P

epsilon = 1e-06
exact = lax.Precision.HIGHEST
LANES = 128
ROWS = 8
PLANES = 4
QUARTERS = 4
CHUNKS = 2


def gray(position):
    return position ^ (position >> 1)


def row_offset(step, mate, position, quarter):
    start = gray((position + step) % PLANES) * (QUARTERS * ROWS) + (quarter ^ mate) * ROWS
    return pl.ds(pl.multiple_of(start, ROWS), ROWS)


def halves(value):
    high = value.astype(jnp.bfloat16)
    return high, (value - high.astype(jnp.float32)).astype(jnp.bfloat16)


def product(weight, value):
    def dot(a, b):
        return lax.dot_general(a, b, (((0,), (0,)), ((), ())), preferred_element_type=jnp.float32)

    weight_high, weight_low = halves(weight)
    value_high, value_low = halves(value)
    return dot(weight_high, value_high) + (dot(weight_high, value_low) + dot(weight_low, value_high))


def pick(piece, index, group):
    kind, base, refs = piece
    if kind == "whole":
        return refs[0][base + index]
    if kind == "halves":
        inside = base + index % 4
        owner = index // 4
    else:
        inside = base + index
        owner = 0 if kind == "next" else 1
    return jnp.where(group == owner, refs[0][inside], refs[1][inside])


def sent_tile(step, index, other, by_piece):
    if by_piece:
        return step, (other * ROWS + index) * ROWS
    return other // 2, ((other % 2) * 32 + step * ROWS + index) * ROWS


class Taker:
    def __init__(self, refs):
        self.refs = list(refs)

    def __call__(self, count):
        head, self.refs = self.refs[:count], self.refs[count:]
        return head


def read_place(place):
    return place[0], place[1], place[2]


def take_weights(take, kinds):
    return [(kind, base, take(1 if kind == "whole" else 2)) for kind, base in kinds]


def first_factor(steps, by_piece, current, gain, weights, send, tile, place):
    position, quarter, group = place
    squares = jnp.zeros((ROWS, LANES), jnp.float32)
    for n, step in enumerate(steps):
        for index in range(ROWS):
            value = current[n][index]
            squares += jnp.sum((value * value).reshape(LANES // ROWS, ROWS, LANES), axis=0)
            tile[index] = product(pick(weights[n], index, group), value * gain[n][index])
        for index in range(ROWS):
            for other in range(PLANES):
                for mate in range(QUARTERS):
                    part, start = sent_tile(step, index, other, by_piece)
                    ref = send[0 if by_piece else part][mate]
                    ref[pl.ds(start, ROWS), :] = tile[index, row_offset(other, mate, position, quarter), :]
    for ref in send[0]:
        ref[pl.ds(ref.shape[0] - ROWS, ROWS), :] = squares


def first_kernel(step, kinds, place, *refs):
    take = Taker(refs)
    tokens = take(1)[0]
    weights = take_weights(take, kinds)
    current, gain, rows, send, tile = take(1), take(1), take(1)[0], [take(QUARTERS)], take(1)[0]
    for index in range(ROWS):
        current[0][index] = tokens[pl.ds(0, LANES), pl.ds(index * LANES, LANES)].T
    rows[...] = tokens[pl.ds(LANES, ROWS), :]
    spread_gain(0, rows, gain[0])
    first_factor([step], True, current, gain, weights, send, tile, read_place(place))


def spread_gain(layer, rows, spread):
    for index in range(ROWS):
        columns = rows[:, pl.ds(index * LANES, LANES)].T
        spread[index] = jnp.broadcast_to(columns[:, layer : layer + 1], (LANES, LANES))


def deal_kernel(rounds, place, tokens, gains, their_tokens, their_gains, *pieces):
    position, core = place[0], place[1] % 2
    half = their_tokens.shape[1]
    columns = pl.ds(pl.multiple_of(core * half, half), half)
    rows = []
    for r in range(rounds):
        mine, other = gains[pl.ds(r, 1), columns], their_gains[pl.ds(r, 1), :]
        rows += [jnp.where(core == 0, mine, other), jnp.where(core == 0, other, mine)]
    rows.append(jnp.zeros((ROWS - 2 * rounds, half), jnp.float32))
    rows = jnp.concatenate(rows)
    for step in range(PLANES):
        plane = gray((position + PLANES - step) % PLANES)
        base = (plane % 2) * LANES

        def move(n, carry, step=step, plane=plane, base=base):
            start = pl.multiple_of(base + n * ROWS, ROWS)
            kept, other = tokens[pl.ds(start, ROWS), columns], their_tokens[pl.ds(start, ROWS), :]
            there = pl.ds(pl.multiple_of(n * ROWS, ROWS), ROWS)
            pieces[step][there, :] = jnp.where(plane // 2 == core, kept, other)
            return carry

        lax.fori_loop(0, LANES // ROWS, move, 0, unroll=4)
        pieces[step][pl.ds(LANES, ROWS), :] = rows


def last_kernel(width, step, squares_count, place, *refs):
    take = Taker(refs)
    position, quarter, _ = read_place(place)
    current, old_gain, squares_in, mixed = take(1)[0], take(1)[0], take(squares_count), take(QUARTERS)
    result, tile = take(2)
    scale = token_scale(width, squares_in)
    for index in range(ROWS):
        for other in range(PLANES):
            for mate in range(QUARTERS):
                where = row_offset(other, mate, position, quarter)
                _, start = sent_tile(step, index, other, True)
                mix = mixed[mate][pl.ds(start, ROWS), :]
                tile[index, where, :] = residual(current[index, where, :], mix, scale, old_gain[index, where, :])
        result[:, pl.ds(index * LANES, LANES)] = tile[index].T


def token_scale(width, squares):
    total = sum(ref[pl.ds(ref.shape[0] - ROWS, ROWS), :] for ref in squares)
    scale = lax.rsqrt(jnp.sum(total, axis=0, keepdims=True) / width + epsilon)
    return jnp.broadcast_to(scale, (ROWS, LANES))


def residual(value, mix, scale, gain):
    normed = value * scale * gain
    return value + (mix * scale) * (normed / (1.0 + jnp.exp(-normed)))


def edge_kernel(width, squares_count, kinds, place, *refs):
    take = Taker(refs)
    position, quarter, group = read_place(place)
    current, old_gain = take(PLANES), take(PLANES)
    squares_in = take(squares_count)
    mixed = [take(QUARTERS) for _ in range(CHUNKS)]
    gain = take(PLANES)
    weights = take_weights(take, kinds)
    fresh = take(PLANES)
    send, tile = [take(QUARTERS) for _ in range(CHUNKS)], take(1)[0]
    scale = token_scale(width, squares_in)
    for step in range(PLANES):

        def finish(index, carry, step=step):
            for other in range(PLANES):
                for mate in range(QUARTERS):
                    where = row_offset(other, mate, position, quarter)
                    value = current[step][index, where, :]
                    part, start = sent_tile(step, index, other, False)
                    mix = mixed[part][mate][pl.ds(pl.multiple_of(start, ROWS), ROWS), :]
                    gained = old_gain[step][index, where, :]
                    fresh[step][index, where, :] = residual(value, mix, scale, gained)
            return carry

        lax.fori_loop(0, ROWS, finish, 0, unroll=2)

    first_factor(range(PLANES), False, fresh, gain, weights, send, tile, (position, quarter, group))


def column_kernel(others, in_pieces, out_pieces, kinds, gain_layer, place, *refs):
    take = Taker(refs)
    position, quarter, group = read_place(place)
    came = [take(QUARTERS) for _ in range(PLANES if in_pieces else len(others) // 2)]
    weights = take_weights(take, kinds)
    rows = take(PLANES) if gain_layer else []
    send = [take(QUARTERS) for _ in range(PLANES if out_pieces else len(others) // 2)]
    spread = take(PLANES) if gain_layer else []
    value, tile = take(2)
    for n, other in enumerate(others):
        for index in range(ROWS):
            for step in range(PLANES):
                for mate in range(QUARTERS):
                    part, start = sent_tile(step, 0, other, in_pieces)
                    ref = came[part if in_pieces else n // 2][mate]
                    value[index, row_offset(step, mate, position, quarter), :] = ref[
                        pl.ds(start + index, ROWS, stride=ROWS), :
                    ]
            tile[index] = product(pick(weights[n], index, group), value[index])
            for step in range(PLANES):
                for mate in range(QUARTERS):
                    part, start = sent_tile(step, 0, other, out_pieces)
                    send[part if out_pieces else n // 2][mate][pl.ds(start + index, ROWS, stride=ROWS), :] = tile[
                        index, row_offset(step, mate, position, quarter), :
                    ]
    for step in range(len(rows)):
        spread_gain(gain_layer, rows[step], spread[step])


SMALL = pl.BlockSpec(memory_space=pltpu.SMEM)
WHOLE = pl.BlockSpec(memory_space=pltpu.VMEM)
PARAMS = pltpu.CompilerParams(vmem_limit_bytes=8 * 1024 * 1024)
PIECE = (ROWS, LANES, LANES)
COST_PART = 16


def array(*shape):
    return jax.ShapeDtypeStruct(shape, jnp.float32)


def marked(kernel, operand_count, wait_count, *refs):
    outs = refs[operand_count + wait_count :]
    outs[0][0] = 0
    kernel(*refs[:operand_count], *outs[1:])


def call(kernel, operands, outs, scratch, flops, waits=(), specs=None, out_spec=WHOLE):
    moved = 4 * (sum(a.size for a in operands) + sum(o.size for o in outs))
    results = pl.pallas_call(
        functools.partial(marked, kernel, len(operands), len(waits)),
        out_shape=[jax.ShapeDtypeStruct((1,), jnp.int32), *outs],
        in_specs=[SMALL] + (specs or [WHOLE] * (len(operands) - 1)) + [WHOLE if w.ndim > 1 else SMALL for w in waits],
        out_specs=[SMALL] + [out_spec] * len(outs),
        scratch_shapes=scratch if isinstance(scratch, list) else [pltpu.VMEM(PIECE, jnp.float32)] * scratch,
        compiler_params=PARAMS,
        cost_estimate=pl.CostEstimate(flops=flops // COST_PART, bytes_accessed=moved // COST_PART, transcendentals=0),
    )(*operands, *waits)
    return list(results[1:]), results[0]


def copies_kernel(moves, in_count, out_count, place, *refs):
    sems = refs[-1]
    copies = []
    for n, (source, at, target, there, when) in enumerate(moves):
        copy = pltpu.make_async_copy(refs[source].at[at(place)], refs[in_count + target].at[there], sems.at[n])
        copies.append((copy, when))
    for act in ("start", "wait"):
        for copy, when in copies:
            if when is None:
                getattr(copy, act)()
            else:
                pl.when(when(place))(getattr(copy, act))


def copied(place, operands, outs, moves, waits=(), anywhere=True):
    specs = [pl.BlockSpec(memory_space=pl.ANY) if anywhere else WHOLE] * len(operands)
    kernel = functools.partial(copies_kernel, moves, len(operands), len(outs))
    sems = [pltpu.SemaphoreType.DMA((len(moves),))]
    return call(kernel, [place, *operands], outs, sems, 0, waits, specs)[0]


def core_of(place):
    return place[1] % 2


STAGE_FLOPS = 6 * 32 * LANES * LANES * LANES


def split_weights(weights):
    return [array for piece in weights for array in piece[2]], [piece[:2] for piece in weights]


def deal(place, tokens, gains, their_tokens, their_gains):
    outs = [array(LANES + ROWS, their_tokens.shape[1])] * PLANES
    operands = [place, tokens, gains, their_tokens, their_gains]
    return call(functools.partial(deal_kernel, gains.shape[0]), operands, outs, 0, 0)


def first_piece(step, place, tokens, weights, waits):
    operands, kinds = split_weights([weights])
    kernel = functools.partial(first_kernel, step, kinds)
    outs = [array(*PIECE)] * 2 + [array(ROWS, ROWS * LANES)] + [array(264, LANES)] * QUARTERS
    results, mark = call(kernel, [place, tokens, *operands], outs, 1, STAGE_FLOPS // 4, waits)
    return results[:3], results[3:], mark


def last_piece(width, step, place, current, old_gain, squares, mixed):
    kernel = functools.partial(last_kernel, width, step, len(squares))
    operands = [place, current, old_gain, *squares, *mixed]
    return call(kernel, operands, [array(LANES, ROWS * LANES)], 1, STAGE_FLOPS // 4)[0][0]


def layer_edge(width, place, current, old_gain, squares, mixed, gain, weights):
    more, kinds = split_weights(weights)
    operands = [place, *current, *old_gain, *squares, *mixed[0], *mixed[1], *gain, *more]
    outs = [array(*PIECE)] * PLANES + [array(520, LANES)] * QUARTERS + [array(512, LANES)] * QUARTERS
    kernel = functools.partial(edge_kernel, width, len(squares), kinds)
    results, mark = call(kernel, operands, outs, 1, 2 * STAGE_FLOPS)
    return results[:PLANES], [results[PLANES : PLANES + QUARTERS], results[PLANES + QUARTERS :]], mark


def column_stage(others, in_pieces, out_pieces, place, came, weights, waits, rows=(), gain_layer=0):
    more, kinds = split_weights(weights)
    operands = [place, *(ref for part in came for ref in part), *more, *rows]
    outs = [array(256, LANES)] * (QUARTERS * PLANES) if out_pieces else [array(512, LANES)] * QUARTERS
    count = len(outs)
    outs = outs + [array(*PIECE)] * len(rows)
    kernel = functools.partial(column_kernel, others, in_pieces, out_pieces, kinds, gain_layer)
    results, mark = call(kernel, operands, outs, 2, STAGE_FLOPS, waits)
    return [results[n : n + QUARTERS] for n in range(0, count, QUARTERS)], results[count:], mark


def routed(value, to):
    route = []
    for core in range(2):
        for z in range(PLANES):
            for y in range(2):
                there = to(core, z, y)
                route.append((core * 8 + z * 2 + y, there[0] * 8 + there[1] * 2 + there[2]))
    return lax.ppermute(value, ("segment", "block"), route)


def core_swap(value):
    return routed(value, lambda core, z, y: (1 - core, z, y))


def ring(value, distance):
    return routed(value, lambda core, z, y: (core, gray((gray(z) + distance) % PLANES), y))


def group_ring(value):
    route = []
    for group in range(2):
        for core in range(2):
            for z in range(PLANES):
                for y in range(2):
                    there = gray((gray(z) + (1 if group else -1)) % PLANES)
                    start = group * 16 + core * 8 + y
                    route.append((start + z * 2, start + there * 2))
    return lax.ppermute(value, ("groups", "segment", "block"), route)


def to_mate(value, mate):
    return routed(value, lambda core, z, y: (core ^ (mate & 1), z, y ^ (mate >> 1)))


def group_swap(value):
    return lax.ppermute(value, "groups", [(0, 1), (1, 0)])


def exchange(chunk):
    return [chunk[0]] + [to_mate(chunk[mate], mate) for mate in range(1, QUARTERS)]


def plane_body(tokens, gains, right_factors, left_factors):
    core = lax.axis_index("segment")
    block = lax.axis_index("block")
    group = lax.axis_index("groups")
    z, y = block // 2, block % 2
    position = gray(z)
    place = jnp.stack([position, y * 2 + core, group]).astype(jnp.int32)
    rounds = right_factors.shape[1]
    layers = 2 * rounds
    width = right_factors.shape[3] * 8 * right_factors.shape[2]

    count, half = tokens.shape[0], tokens.shape[1] // 2
    their_tokens = core_swap(lax.dynamic_slice_in_dim(tokens, (1 - core) * half, half, 1))
    their_gains = core_swap(lax.dynamic_slice_in_dim(gains[0], (1 - core) * half, half, 1))

    pieces, dealt = deal(place, tokens, gains[0], their_tokens, their_gains)
    arrived = [piece if step == 0 else ring(piece, -step) for step, piece in enumerate(pieces)]

    def swapped(factors, r, waits):
        move = (0, lambda p: (0, r, pl.ds((1 - core_of(p)) * ROWS, ROWS)), 0, pl.ds(0, ROWS), None)
        return factors, r, core_swap(copied(place, [factors], [array(*PIECE)], [move], waits)[0])

    def own(pairs, section, waits):
        operands, moves = [], []
        for n, (factors, r, theirs) in enumerate(pairs):
            there = pl.ds(n * ROWS, ROWS)
            operands += [factors, theirs]
            mine = lambda p, r=r: (0, r, pl.ds(core_of(p) * ROWS, ROWS))
            moves.append((2 * n, mine, 0, there, lambda p: core_of(p) == section))
            moves.append((2 * n + 1, lambda p: pl.ds(0, ROWS), 0, there, lambda p: core_of(p) != section))
        return copied(place, operands, [array(len(pairs) * ROWS, LANES, LANES)], moves, waits)[0]

    def near_half(near, waits=()):
        count = near.shape[0] // ROWS
        moves = [
            (0, lambda p, n=n: pl.ds(n * ROWS + p[2] * 4, 4), 0, pl.ds(n * 4, 4), None) for n in range(count)
        ]
        moves.append((0, lambda p: pl.ds(0, count * ROWS), 1, pl.ds(0, count * ROWS), None))
        outs = [array(count * 4, LANES, LANES), array(count * ROWS, LANES, LANES)]
        passed, kept = copied(place, [near], outs, moves, waits, False)
        return group_ring(passed), kept

    def near_halves(near, waits):
        moves, outs = [], []
        for n in range(2):
            moves.append((0, lambda p, n=n: pl.ds(n * ROWS + p[2] * 4, 4), 2 * n, pl.ds(0, 4), None))
            moves.append((0, lambda p, n=n: pl.ds(n * ROWS, ROWS), 2 * n + 1, pl.ds(0, ROWS), None))
            outs += [array(4, LANES, LANES), array(*PIECE)]
        passed, kept, left_passed, left_kept = copied(place, [near], outs, moves, waits, False)
        return (group_ring(passed), kept), (group_ring(left_passed), left_kept)

    def apart(part, n, far, near):
        near_pair, far_pair = (near, group_swap(near)), (far, group_swap(far))
        return [("whole", n * ROWS, (part,)), ("next", 0, near_pair), ("halves", 0, far_pair), ("previous", 0, near_pair)]

    def four_pieces(part, far, near):
        near_pair, far_pair = (near, group_swap(near)), (far, group_swap(far))
        return [
            [
                ("whole", n * ROWS, (part,)),
                ("next", n * ROWS, near_pair),
                ("halves", n * 4, far_pair),
                ("previous", n * ROWS, near_pair),
            ]
            for n in range(part.shape[0] // ROWS)
        ]

    right_parts, left_parts = [None] * layers, [None] * layers
    pairs = [swapped(right_factors, 0, ())]
    part = own(pairs, 0, ())
    near = group_ring(part)
    pairs.append(swapped(left_factors, 0, [dealt]))

    current, gain, rows, came = [None] * PLANES, [None] * PLANES, [None] * PLANES, [None] * PLANES
    waits = []
    near_pair = near, group_swap(near)
    for step in (0, 1, 3, 2):
        weights = [("whole", 0, (part,)), ("next", 0, near_pair), None, ("previous", 0, near_pair)][step]
        if step == 2:
            weights = ("halves", 0, (far, group_swap(far)))
        results, sends, mark = first_piece(step, place, arrived[step], weights, waits)
        waits = [mark]
        current[step], gain[step], rows[step] = results
        came[step] = exchange(sends)
        if step == 1:
            far, _ = near_half(near, [*arrived[1:], mark])
        if step == 3:
            left = own(pairs[1:], 0, [arrived[2], mark, *came[0][2:], *came[1][2:]])
            left_near = group_ring(left)
    far, near = near_half(left_near, [mark, *came[3][2:]])
    (left_parts[0],) = four_pieces(left, far, near)
    right = own(pairs[:1], 1, [far, *came[2][2:]])
    right_near = group_ring(right)
    left = own(pairs[1:], 1, [right, left_parts[0][1][2][1]])
    left_near = group_ring(left)
    for layer in range(layers - 1):
        in_pieces = layer == 0
        squares = [part[mate] for part in (came if in_pieces else came[:1]) for mate in range(QUARTERS)]
        mixed, marks = [], []
        for chunk in range(CHUNKS):
            others = (chunk * 2, chunk * 2 + 1)
            extra = (rows, layer + 1) if chunk == 0 else ()
            weights = left_parts[layer][others[0] : others[1] + 1]
            source = came if in_pieces else came[chunk : chunk + 1]
            (half_sends,), spread, mark = column_stage(
                others, in_pieces, False, place, source, weights, marks, *extra
            )
            mixed.append(exchange(half_sends))
            marks = [mark]
            next_gain = spread or next_gain
        if layer == 0:
            far, near = near_half(right_near, marks)
            (right_parts[1],) = four_pieces(right, far, near)
            right_last = [right_parts[1][2][2][1]]
            far, near = near_half(left_near, [far, right_parts[1][1][2][1], *mixed[0][2:]])
            (left_parts[1],) = four_pieces(left, far, near)
            pairs = [swapped(factors, 1, marks) for factors in (right_factors, left_factors)]
        if layer == 2:
            far, _ = near_half(near, marks)
            right_parts[3], left_parts[3] = four_pieces(part, far, near)
        if layer + 2 < layers:
            waits = [far, *right_last, *mixed[0][2:], *mixed[1][2:]]
            part = own(pairs, layer % 2, waits)
            near = group_ring(part)
        current, sends, mark = layer_edge(
            width, place, current, gain, squares, mixed, next_gain, right_parts[layer + 1]
        )
        gain = next_gain
        came = [exchange(sends[0]), exchange(sends[1])]
        if layer + 2 < layers:
            if layer == 0:
                swaps = left_parts[1][1][2][1], left_parts[1][2][2][1]
                moved = near_halves(near, [mark, *came[0][2:], *swaps])
                right_parts[2], left_parts[2] = [apart(part, n, *moved[n]) for n in range(2)]
                far, right_last = moved[1][0], [right_parts[2][n][2][1] for n in (1, 2)]

    squares = came[0]
    sends, _, _ = column_stage(tuple(range(PLANES)), False, True, place, came, left_parts[-1], ())
    back = [None] * PLANES
    for step in (2, 1, 3, 0):
        mixed = exchange(sends[step])
        done = last_piece(width, step, place, current[step], gain[step], squares, mixed)
        back[step] = done if step == 0 else ring(done, step)
    stacked = jnp.stack(back)

    def found_for(half_index):
        planes = [half_index * 2 + n for n in range(2)]
        return jnp.stack(
            [lax.dynamic_index_in_dim(stacked, (position - gray(p)) % PLANES, 0, keepdims=False) for p in planes]
        ).reshape(tokens.shape[0], half)

    mine = found_for(core)
    theirs = core_swap(found_for(1 - core))
    return jnp.where(core == 0, jnp.concatenate([mine, theirs], 1), jnp.concatenate([theirs, mine], 1))


def wide_body(tokens, gains, right_factors, left_factors):
    blocks_here, block_size = right_factors.shape[2:4]
    token_count, width_here = tokens.shape
    width = width_here * lax.axis_size("block")
    rounds = right_factors.shape[1]
    core = lax.axis_index("segment")
    count = lax.axis_size("segment")

    def gathered(value):
        return lax.all_gather(value[0], "segment", axis=0)

    gains, right_factors, left_factors = gathered(gains), gathered(right_factors), gathered(left_factors)
    current = tokens.T
    for layer in range(count * rounds):
        s, r = layer % count, layer // count
        sum_squares = lax.psum(jnp.sum(current * current, axis=0), "block")
        normed = current * lax.rsqrt(sum_squares / width + epsilon)[None, :] * gains[s, r][:, None]
        inner = jnp.einsum(
            "bit,bij->bjt",
            normed.reshape(blocks_here, block_size, token_count),
            right_factors[s, r],
            precision=exact,
        )
        combined = jnp.einsum(
            "bjt,jbc->cjt",
            lax.all_to_all(inner, "block", split_axis=1, concat_axis=0, tiled=True),
            left_factors[s, r],
            precision=exact,
        )
        mixed = lax.all_to_all(combined, "block", split_axis=0, concat_axis=1, tiled=True)
        current = current + mixed.reshape(width_here, token_count) * jax.nn.silu(normed)
    return current.T


def solution(mesh):
    placed = (
        P(("groups", "segment"), "block"),
        P("segment", None, "block"),
        P("segment", None, "block", None, None),
        P("segment", None, "block", None, None),
    )
    planes = dict(mesh.shape) == {"groups": 2, "segment": 2, "block": 8}

    def body(tokens, gains, right_factors, left_factors):
        fits = planes and tokens.shape == (256, 2048) and right_factors.shape[2:] == (16, 128, 128)
        return (plane_body if fits else wide_body)(tokens, gains, right_factors, left_factors)

    return jax.shard_map(
        body,
        mesh=mesh,
        in_specs=placed,
        out_specs=P(("groups", "segment"), "block"),
        check_vma=False,
    )
```

```python
import functools

import jax
import jax.numpy as jnp
from jax import lax
from jax.experimental import pallas as pl
from jax.experimental.pallas import tpu as pltpu
from jax.sharding import PartitionSpec as P

epsilon = 1e-06
exact = lax.Precision.HIGHEST
LANES = 128
ROWS = 8
PLANES = 4
QUARTERS = 4
CHUNKS = 2


def gray(position):
    return position ^ (position >> 1)


def row_offset(step, mate, position, quarter):
    start = gray((position + step) % PLANES) * (QUARTERS * ROWS) + (quarter ^ mate) * ROWS
    return pl.ds(pl.multiple_of(start, ROWS), ROWS)


def halves(value):
    high = value.astype(jnp.bfloat16)
    return high, (value - high.astype(jnp.float32)).astype(jnp.bfloat16)


def product(weight, value):
    def dot(a, b):
        return lax.dot_general(a, b, (((0,), (0,)), ((), ())), preferred_element_type=jnp.float32)

    weight_high, weight_low = halves(weight)
    value_high, value_low = halves(value)
    return dot(weight_high, value_high) + (dot(weight_high, value_low) + dot(weight_low, value_high))


def pick(piece, index, group):
    kind, base, refs = piece
    if kind == "whole":
        return refs[0][base + index]
    if kind == "halves":
        inside = base + index % 4
        owner = index // 4
    else:
        inside = base + index
        owner = 0 if kind == "next" else 1
    return jnp.where(group == owner, refs[0][inside], refs[1][inside])


def sent_tile(step, index, other, by_piece):
    if by_piece:
        return step, (other * ROWS + index) * ROWS
    return other // 2, ((other % 2) * 32 + step * ROWS + index) * ROWS


class Taker:
    def __init__(self, refs):
        self.refs = list(refs)

    def __call__(self, count):
        head, self.refs = self.refs[:count], self.refs[count:]
        return head


def read_place(place):
    return place[0], place[1], place[2]


def take_weights(take, kinds):
    return [(kind, base, take(1 if kind == "whole" else 2)) for kind, base in kinds]


def first_factor(steps, by_piece, current, gain, weights, send, tile, place):
    position, quarter, group = place
    squares = jnp.zeros((ROWS, LANES), jnp.float32)
    for n, step in enumerate(steps):
        for index in range(ROWS):
            value = current[n][index]
            squares += jnp.sum((value * value).reshape(LANES // ROWS, ROWS, LANES), axis=0)
            tile[index] = product(pick(weights[n], index, group), value * gain[n][index])
        for index in range(ROWS):
            for other in range(PLANES):
                for mate in range(QUARTERS):
                    part, start = sent_tile(step, index, other, by_piece)
                    ref = send[0 if by_piece else part][mate]
                    ref[pl.ds(start, ROWS), :] = tile[index, row_offset(other, mate, position, quarter), :]
    for ref in send[0]:
        ref[pl.ds(ref.shape[0] - ROWS, ROWS), :] = squares


def first_kernel(step, kinds, place, *refs):
    take = Taker(refs)
    tokens = take(1)[0]
    weights = take_weights(take, kinds)
    current, gain, rows, send, tile = take(1), take(1), take(1)[0], [take(QUARTERS)], take(1)[0]
    for index in range(ROWS):
        current[0][index] = tokens[pl.ds(0, LANES), pl.ds(index * LANES, LANES)].T
    rows[...] = tokens[pl.ds(LANES, ROWS), :]
    spread_gain(0, rows, gain[0])
    first_factor([step], True, current, gain, weights, send, tile, read_place(place))


def spread_gain(layer, rows, spread):
    for index in range(ROWS):
        columns = rows[:, pl.ds(index * LANES, LANES)].T
        spread[index] = jnp.broadcast_to(columns[:, layer : layer + 1], (LANES, LANES))


def deal_kernel(rounds, place, tokens, gains, their_tokens, their_gains, *pieces):
    position, core = place[0], place[1] % 2
    half = their_tokens.shape[1]
    columns = pl.ds(pl.multiple_of(core * half, half), half)
    rows = []
    for r in range(rounds):
        mine, other = gains[pl.ds(r, 1), columns], their_gains[pl.ds(r, 1), :]
        rows += [jnp.where(core == 0, mine, other), jnp.where(core == 0, other, mine)]
    rows.append(jnp.zeros((ROWS - 2 * rounds, half), jnp.float32))
    rows = jnp.concatenate(rows)
    for step in range(PLANES):
        plane = gray((position + PLANES - step) % PLANES)
        base = (plane % 2) * LANES

        def move(n, carry, step=step, plane=plane, base=base):
            start = pl.multiple_of(base + n * ROWS, ROWS)
            kept, other = tokens[pl.ds(start, ROWS), columns], their_tokens[pl.ds(start, ROWS), :]
            there = pl.ds(pl.multiple_of(n * ROWS, ROWS), ROWS)
            pieces[step][there, :] = jnp.where(plane // 2 == core, kept, other)
            return carry

        lax.fori_loop(0, LANES // ROWS, move, 0, unroll=4)
        pieces[step][pl.ds(LANES, ROWS), :] = rows


def last_kernel(width, step, squares_count, place, *refs):
    take = Taker(refs)
    position, quarter, _ = read_place(place)
    current, old_gain, squares_in, mixed = take(1)[0], take(1)[0], take(squares_count), take(QUARTERS)
    result, tile = take(2)
    scale = token_scale(width, squares_in)
    for index in range(ROWS):
        for other in range(PLANES):
            for mate in range(QUARTERS):
                where = row_offset(other, mate, position, quarter)
                _, start = sent_tile(step, index, other, True)
                mix = mixed[mate][pl.ds(start, ROWS), :]
                tile[index, where, :] = residual(current[index, where, :], mix, scale, old_gain[index, where, :])
        result[:, pl.ds(index * LANES, LANES)] = tile[index].T


def token_scale(width, squares):
    total = sum(ref[pl.ds(ref.shape[0] - ROWS, ROWS), :] for ref in squares)
    scale = lax.rsqrt(jnp.sum(total, axis=0, keepdims=True) / width + epsilon)
    return jnp.broadcast_to(scale, (ROWS, LANES))


def residual(value, mix, scale, gain):
    normed = value * scale * gain
    return value + (mix * scale) * (normed / (1.0 + jnp.exp(-normed)))


def edge_kernel(width, squares_count, kinds, place, *refs):
    take = Taker(refs)
    position, quarter, group = read_place(place)
    current, old_gain = take(PLANES), take(PLANES)
    squares_in = take(squares_count)
    mixed = [take(QUARTERS) for _ in range(CHUNKS)]
    gain = take(PLANES)
    weights = take_weights(take, kinds)
    fresh = take(PLANES)
    send, tile = [take(QUARTERS) for _ in range(CHUNKS)], take(1)[0]
    scale = token_scale(width, squares_in)
    for step in range(PLANES):

        def finish(index, carry, step=step):
            for other in range(PLANES):
                for mate in range(QUARTERS):
                    where = row_offset(other, mate, position, quarter)
                    value = current[step][index, where, :]
                    part, start = sent_tile(step, index, other, False)
                    mix = mixed[part][mate][pl.ds(pl.multiple_of(start, ROWS), ROWS), :]
                    gained = old_gain[step][index, where, :]
                    fresh[step][index, where, :] = residual(value, mix, scale, gained)
            return carry

        lax.fori_loop(0, ROWS, finish, 0, unroll=2)

    first_factor(range(PLANES), False, fresh, gain, weights, send, tile, (position, quarter, group))


def column_kernel(others, in_pieces, out_pieces, kinds, gain_layer, place, *refs):
    take = Taker(refs)
    position, quarter, group = read_place(place)
    came = [take(QUARTERS) for _ in range(PLANES if in_pieces else len(others) // 2)]
    weights = take_weights(take, kinds)
    rows = take(PLANES) if gain_layer else []
    send = [take(QUARTERS) for _ in range(PLANES if out_pieces else len(others) // 2)]
    spread = take(PLANES) if gain_layer else []
    value, tile = take(2)
    for n, other in enumerate(others):
        for index in range(ROWS):
            for step in range(PLANES):
                for mate in range(QUARTERS):
                    part, start = sent_tile(step, 0, other, in_pieces)
                    ref = came[part if in_pieces else n // 2][mate]
                    value[index, row_offset(step, mate, position, quarter), :] = ref[
                        pl.ds(start + index, ROWS, stride=ROWS), :
                    ]
            tile[index] = product(pick(weights[n], index, group), value[index])
            for step in range(PLANES):
                for mate in range(QUARTERS):
                    part, start = sent_tile(step, 0, other, out_pieces)
                    send[part if out_pieces else n // 2][mate][pl.ds(start + index, ROWS, stride=ROWS), :] = tile[
                        index, row_offset(step, mate, position, quarter), :
                    ]
    for step in range(len(rows)):
        spread_gain(gain_layer, rows[step], spread[step])


SMALL = pl.BlockSpec(memory_space=pltpu.SMEM)
WHOLE = pl.BlockSpec(memory_space=pltpu.VMEM)
PARAMS = pltpu.CompilerParams(vmem_limit_bytes=8 * 1024 * 1024)
PIECE = (ROWS, LANES, LANES)
COST_PART = 16


def array(*shape):
    return jax.ShapeDtypeStruct(shape, jnp.float32)


def marked(kernel, operand_count, wait_count, *refs):
    outs = refs[operand_count + wait_count :]
    outs[0][0] = 0
    kernel(*refs[:operand_count], *outs[1:])


def call(kernel, operands, outs, scratch, flops, waits=(), specs=None, out_spec=WHOLE):
    moved = 4 * (sum(a.size for a in operands) + sum(o.size for o in outs))
    results = pl.pallas_call(
        functools.partial(marked, kernel, len(operands), len(waits)),
        out_shape=[jax.ShapeDtypeStruct((1,), jnp.int32), *outs],
        in_specs=[SMALL] + (specs or [WHOLE] * (len(operands) - 1)) + [WHOLE if w.ndim > 1 else SMALL for w in waits],
        out_specs=[SMALL] + [out_spec] * len(outs),
        scratch_shapes=scratch if isinstance(scratch, list) else [pltpu.VMEM(PIECE, jnp.float32)] * scratch,
        compiler_params=PARAMS,
        cost_estimate=pl.CostEstimate(flops=flops // COST_PART, bytes_accessed=moved // COST_PART, transcendentals=0),
    )(*operands, *waits)
    return list(results[1:]), results[0]


def copies_kernel(moves, in_count, out_count, place, *refs):
    sems = refs[-1]
    copies = []
    for n, (source, at, target, there, when) in enumerate(moves):
        copy = pltpu.make_async_copy(refs[source].at[at(place)], refs[in_count + target].at[there], sems.at[n])
        copies.append((copy, when))
    for act in ("start", "wait"):
        for copy, when in copies:
            if when is None:
                getattr(copy, act)()
            else:
                pl.when(when(place))(getattr(copy, act))


def copied(place, operands, outs, moves, waits=(), anywhere=True):
    specs = [pl.BlockSpec(memory_space=pl.ANY) if anywhere else WHOLE] * len(operands)
    kernel = functools.partial(copies_kernel, moves, len(operands), len(outs))
    sems = [pltpu.SemaphoreType.DMA((len(moves),))]
    return call(kernel, [place, *operands], outs, sems, 0, waits, specs)[0]


def core_of(place):
    return place[1] % 2


STAGE_FLOPS = 6 * 32 * LANES * LANES * LANES


def split_weights(weights):
    return [array for piece in weights for array in piece[2]], [piece[:2] for piece in weights]


def deal(place, tokens, gains, their_tokens, their_gains):
    outs = [array(LANES + ROWS, their_tokens.shape[1])] * PLANES
    operands = [place, tokens, gains, their_tokens, their_gains]
    return call(functools.partial(deal_kernel, gains.shape[0]), operands, outs, 0, 0)


def first_piece(step, place, tokens, weights, waits):
    operands, kinds = split_weights([weights])
    kernel = functools.partial(first_kernel, step, kinds)
    outs = [array(*PIECE)] * 2 + [array(ROWS, ROWS * LANES)] + [array(264, LANES)] * QUARTERS
    results, mark = call(kernel, [place, tokens, *operands], outs, 1, STAGE_FLOPS // 4, waits)
    return results[:3], results[3:], mark


def last_piece(width, step, place, current, old_gain, squares, mixed):
    kernel = functools.partial(last_kernel, width, step, len(squares))
    operands = [place, current, old_gain, *squares, *mixed]
    return call(kernel, operands, [array(LANES, ROWS * LANES)], 1, STAGE_FLOPS // 4)[0][0]


def layer_edge(width, place, current, old_gain, squares, mixed, gain, weights):
    more, kinds = split_weights(weights)
    operands = [place, *current, *old_gain, *squares, *mixed[0], *mixed[1], *gain, *more]
    outs = [array(*PIECE)] * PLANES + [array(520, LANES)] * QUARTERS + [array(512, LANES)] * QUARTERS
    kernel = functools.partial(edge_kernel, width, len(squares), kinds)
    results, mark = call(kernel, operands, outs, 1, 2 * STAGE_FLOPS)
    return results[:PLANES], [results[PLANES : PLANES + QUARTERS], results[PLANES + QUARTERS :]], mark


def column_stage(others, in_pieces, out_pieces, place, came, weights, waits, rows=(), gain_layer=0):
    more, kinds = split_weights(weights)
    operands = [place, *(ref for part in came for ref in part), *more, *rows]
    outs = [array(256, LANES)] * (QUARTERS * PLANES) if out_pieces else [array(512, LANES)] * QUARTERS
    count = len(outs)
    outs = outs + [array(*PIECE)] * len(rows)
    kernel = functools.partial(column_kernel, others, in_pieces, out_pieces, kinds, gain_layer)
    results, mark = call(kernel, operands, outs, 2, STAGE_FLOPS, waits)
    return [results[n : n + QUARTERS] for n in range(0, count, QUARTERS)], results[count:], mark


def routed(value, to):
    route = []
    for core in range(2):
        for z in range(PLANES):
            for y in range(2):
                there = to(core, z, y)
                route.append((core * 8 + z * 2 + y, there[0] * 8 + there[1] * 2 + there[2]))
    return lax.ppermute(value, ("segment", "block"), route)


def core_swap(value):
    return routed(value, lambda core, z, y: (1 - core, z, y))


def ring(value, distance):
    return routed(value, lambda core, z, y: (core, gray((gray(z) + distance) % PLANES), y))


def group_ring(value):
    route = []
    for group in range(2):
        for core in range(2):
            for z in range(PLANES):
                for y in range(2):
                    there = gray((gray(z) + (1 if group else -1)) % PLANES)
                    start = group * 16 + core * 8 + y
                    route.append((start + z * 2, start + there * 2))
    return lax.ppermute(value, ("groups", "segment", "block"), route)


def to_mate(value, mate):
    return routed(value, lambda core, z, y: (core ^ (mate & 1), z, y ^ (mate >> 1)))


def group_swap(value):
    return lax.ppermute(value, "groups", [(0, 1), (1, 0)])


def exchange(chunk):
    return [chunk[0]] + [to_mate(chunk[mate], mate) for mate in range(1, QUARTERS)]


def plane_body(tokens, gains, right_factors, left_factors):
    core = lax.axis_index("segment")
    block = lax.axis_index("block")
    group = lax.axis_index("groups")
    z, y = block // 2, block % 2
    position = gray(z)
    place = jnp.stack([position, y * 2 + core, group]).astype(jnp.int32)
    rounds = right_factors.shape[1]
    layers = 2 * rounds
    width = right_factors.shape[3] * 8 * right_factors.shape[2]

    count, half = tokens.shape[0], tokens.shape[1] // 2
    their_tokens = core_swap(lax.dynamic_slice_in_dim(tokens, (1 - core) * half, half, 1))
    their_gains = core_swap(lax.dynamic_slice_in_dim(gains[0], (1 - core) * half, half, 1))

    pieces, dealt = deal(place, tokens, gains[0], their_tokens, their_gains)
    arrived = [piece if step == 0 else ring(piece, -step) for step, piece in enumerate(pieces)]

    def swapped(factors, r, waits):
        move = (0, lambda p: (0, r, pl.ds((1 - core_of(p)) * ROWS, ROWS)), 0, pl.ds(0, ROWS), None)
        return factors, r, core_swap(copied(place, [factors], [array(*PIECE)], [move], waits)[0])

    def own(pairs, section, waits):
        operands, moves = [], []
        for n, (factors, r, theirs) in enumerate(pairs):
            there = pl.ds(n * ROWS, ROWS)
            operands += [factors, theirs]
            mine = lambda p, r=r: (0, r, pl.ds(core_of(p) * ROWS, ROWS))
            moves.append((2 * n, mine, 0, there, lambda p: core_of(p) == section))
            moves.append((2 * n + 1, lambda p: pl.ds(0, ROWS), 0, there, lambda p: core_of(p) != section))
        return copied(place, operands, [array(len(pairs) * ROWS, LANES, LANES)], moves, waits)[0]

    def near_half(near, waits=()):
        count = near.shape[0] // ROWS
        moves = [
            (0, lambda p, n=n: pl.ds(n * ROWS + p[2] * 4, 4), 0, pl.ds(n * 4, 4), None) for n in range(count)
        ]
        moves.append((0, lambda p: pl.ds(0, count * ROWS), 1, pl.ds(0, count * ROWS), None))
        outs = [array(count * 4, LANES, LANES), array(count * ROWS, LANES, LANES)]
        passed, kept = copied(place, [near], outs, moves, waits, False)
        return group_ring(passed), kept

    def near_halves(near, waits):
        moves, outs = [], []
        for n in range(2):
            moves.append((0, lambda p, n=n: pl.ds(n * ROWS + p[2] * 4, 4), 2 * n, pl.ds(0, 4), None))
            moves.append((0, lambda p, n=n: pl.ds(n * ROWS, ROWS), 2 * n + 1, pl.ds(0, ROWS), None))
            outs += [array(4, LANES, LANES), array(*PIECE)]
        passed, kept, left_passed, left_kept = copied(place, [near], outs, moves, waits, False)
        return (group_ring(passed), kept), (group_ring(left_passed), left_kept)

    def apart(part, n, far, near):
        near_pair, far_pair = (near, group_swap(near)), (far, group_swap(far))
        return [("whole", n * ROWS, (part,)), ("next", 0, near_pair), ("halves", 0, far_pair), ("previous", 0, near_pair)]

    def four_pieces(part, far, near):
        near_pair, far_pair = (near, group_swap(near)), (far, group_swap(far))
        return [
            [
                ("whole", n * ROWS, (part,)),
                ("next", n * ROWS, near_pair),
                ("halves", n * 4, far_pair),
                ("previous", n * ROWS, near_pair),
            ]
            for n in range(part.shape[0] // ROWS)
        ]

    right_parts, left_parts = [None] * layers, [None] * layers
    pairs = [swapped(right_factors, 0, ())]
    part = own(pairs, 0, ())
    near = group_ring(part)
    pairs.append(swapped(left_factors, 0, [dealt]))

    current, gain, rows, came = [None] * PLANES, [None] * PLANES, [None] * PLANES, [None] * PLANES
    waits = []
    near_pair = near, group_swap(near)
    for step in (0, 1, 3, 2):
        weights = [("whole", 0, (part,)), ("next", 0, near_pair), None, ("previous", 0, near_pair)][step]
        if step == 2:
            weights = ("halves", 0, (far, group_swap(far)))
        results, sends, mark = first_piece(step, place, arrived[step], weights, waits)
        waits = [mark]
        current[step], gain[step], rows[step] = results
        came[step] = exchange(sends)
        if step == 1:
            far, _ = near_half(near, [*arrived[1:], mark])
        if step == 3:
            left = own(pairs[1:], 0, [arrived[2], mark, *came[0][2:], *came[1][2:]])
            left_near = group_ring(left)
    far, near = near_half(left_near, [mark, *came[3][2:]])
    (left_parts[0],) = four_pieces(left, far, near)
    right = own(pairs[:1], 1, [far, *came[2][2:]])
    right_near = group_ring(right)
    left = own(pairs[1:], 1, [right, left_parts[0][1][2][1]])
    left_near = group_ring(left)
    for layer in range(layers - 1):
        in_pieces = layer == 0
        squares = [part[mate] for part in (came if in_pieces else came[:1]) for mate in range(QUARTERS)]
        mixed, marks = [], []
        for chunk in range(CHUNKS):
            others = (chunk * 2, chunk * 2 + 1)
            extra = (rows, layer + 1) if chunk == 0 else ()
            weights = left_parts[layer][others[0] : others[1] + 1]
            source = came if in_pieces else came[chunk : chunk + 1]
            (half_sends,), spread, mark = column_stage(
                others, in_pieces, False, place, source, weights, marks, *extra
            )
            mixed.append(exchange(half_sends))
            marks = [mark]
            next_gain = spread or next_gain
        if layer == 0:
            far, near = near_half(right_near, marks)
            (right_parts[1],) = four_pieces(right, far, near)
            right_last = [right_parts[1][2][2][1]]
            far, near = near_half(left_near, [far, right_parts[1][1][2][1], *mixed[0][2:]])
            (left_parts[1],) = four_pieces(left, far, near)
            pairs = [swapped(factors, 1, marks) for factors in (right_factors, left_factors)]
        if layer == 2:
            moved = near_halves(near, marks)
            right_parts[3], left_parts[3] = [apart(part, n, *moved[n]) for n in range(2)]
        if layer + 2 < layers:
            waits = [far, *right_last, *mixed[0][2:], *mixed[1][2:]]
            part = own(pairs, layer % 2, waits)
            near = group_ring(part)
        current, sends, mark = layer_edge(
            width, place, current, gain, squares, mixed, next_gain, right_parts[layer + 1]
        )
        gain = next_gain
        came = [exchange(sends[0]), exchange(sends[1])]
        if layer + 2 < layers:
            if layer == 0:
                swaps = left_parts[1][1][2][1], left_parts[1][2][2][1]
                moved = near_halves(near, [mark, *came[0][2:], *swaps])
                right_parts[2], left_parts[2] = [apart(part, n, *moved[n]) for n in range(2)]
                far, right_last = moved[1][0], [right_parts[2][n][2][1] for n in (1, 2)]

    squares = came[0]
    sends, _, _ = column_stage(tuple(range(PLANES)), False, True, place, came, left_parts[-1], ())
    back = [None] * PLANES
    for step in (2, 1, 3, 0):
        mixed = exchange(sends[step])
        done = last_piece(width, step, place, current[step], gain[step], squares, mixed)
        back[step] = done if step == 0 else ring(done, step)
    stacked = jnp.stack(back)

    def found_for(half_index):
        planes = [half_index * 2 + n for n in range(2)]
        return jnp.stack(
            [lax.dynamic_index_in_dim(stacked, (position - gray(p)) % PLANES, 0, keepdims=False) for p in planes]
        ).reshape(tokens.shape[0], half)

    mine = found_for(core)
    theirs = core_swap(found_for(1 - core))
    return jnp.where(core == 0, jnp.concatenate([mine, theirs], 1), jnp.concatenate([theirs, mine], 1))


def wide_body(tokens, gains, right_factors, left_factors):
    blocks_here, block_size = right_factors.shape[2:4]
    token_count, width_here = tokens.shape
    width = width_here * lax.axis_size("block")
    rounds = right_factors.shape[1]
    core = lax.axis_index("segment")
    count = lax.axis_size("segment")

    def gathered(value):
        return lax.all_gather(value[0], "segment", axis=0)

    gains, right_factors, left_factors = gathered(gains), gathered(right_factors), gathered(left_factors)
    current = tokens.T
    for layer in range(count * rounds):
        s, r = layer % count, layer // count
        sum_squares = lax.psum(jnp.sum(current * current, axis=0), "block")
        normed = current * lax.rsqrt(sum_squares / width + epsilon)[None, :] * gains[s, r][:, None]
        inner = jnp.einsum(
            "bit,bij->bjt",
            normed.reshape(blocks_here, block_size, token_count),
            right_factors[s, r],
            precision=exact,
        )
        combined = jnp.einsum(
            "bjt,jbc->cjt",
            lax.all_to_all(inner, "block", split_axis=1, concat_axis=0, tiled=True),
            left_factors[s, r],
            precision=exact,
        )
        mixed = lax.all_to_all(combined, "block", split_axis=0, concat_axis=1, tiled=True)
        current = current + mixed.reshape(width_here, token_count) * jax.nn.silu(normed)
    return current.T


def solution(mesh):
    placed = (
        P(("groups", "segment"), "block"),
        P("segment", None, "block"),
        P("segment", None, "block", None, None),
        P("segment", None, "block", None, None),
    )
    planes = dict(mesh.shape) == {"groups": 2, "segment": 2, "block": 8}

    def body(tokens, gains, right_factors, left_factors):
        fits = planes and tokens.shape == (256, 2048) and right_factors.shape[2:] == (16, 128, 128)
        return (plane_body if fits else wide_body)(tokens, gains, right_factors, left_factors)

    return jax.shard_map(
        body,
        mesh=mesh,
        in_specs=placed,
        out_specs=P(("groups", "segment"), "block"),
        check_vma=False,
    )
```
